128 devices in a mesh: day: 2 (over core), region: 16 (over y, x), scen: 4 (over z).
Axes of the slice: x: 4, y: 4, z: 4, core: 2. Of those that a mesh axis runs over, the one named last changes fastest.
Arguments:
- shipments_init: float32 [4, 16, 16, 128, 2, 256], P('scen', 'region', None, None, 'day'), may hold values from 0 to 1
- holdings_init: float32 [4, 1600, 2, 6, 256], P('scen', 'region', 'day'), may hold values from 0 to 2
- selling_init: float32 [4, 1600, 2, 6, 256], P('scen', 'region', 'day'), may hold values from 0 to 1
- shortage_init: float32 [4, 1600, 2, 256], P('scen', 'region', 'day'), may hold values from 0 to 1
- ordering_init: float32 [240, 256], P('region'), may hold values from 0 to 20
- balance_dual_init: float32 [4, 1600, 2, 6, 256], P('scen', 'region', 'day'), may hold values from -3 to 3
- demand_dual_init: float32 [4, 1600, 2, 256], P('scen', 'region', 'day'), may hold values from -3 to 3
- depot_dual_init: float32 [4, 240, 2, 256], P('scen', 'region', 'day'), may hold values from 0 to 0.1
- demand_base: float32 [1600, 256], P('region'), may hold values from 0.5 to 2
- demand_pattern: float32 [16, 256], replicated, may hold values from 0.5 to 2
- demand_index: int32 [4, 1600, 2], P('scen', 'region', 'day'), may hold values from 0 to 15
- initial_stock: float32 [1600, 5, 256], P('region'), may hold values from 0 to 2
- depot_supply: float32 [240, 2, 256], P('region', 'day'), may hold values from 4 to 16
- lane_cost: float32 [16, 16, 128], replicated, may hold values from 0.1 to 1
- item_volume: float32 [256], replicated, may hold values from 0.5 to 2
- holding_cost: float32 [6, 256], replicated, may hold values from 0.05 to 0.5
- unit_price: float32 [256], replicated, may hold values from 1 to 4
- short_penalty: float32 [256], replicated, may hold values from 2 to 8
- order_cost: float32 [256], replicated, may hold values from 0.5 to 2
- lane_depot: int32 [16, 16, 128], replicated, may hold values from 0 to 14
- lane_store: int32 [16, 16, 128], replicated, may hold values from 0 to 99
- lane_mask: int32 [16, 16, 128], replicated, may hold values 0 or 1
Outputs:
- shipments: float32 [4, 16, 16, 128, 2, 256], P('scen', 'region', None, None, 'day')
- holdings: float32 [4, 1600, 2, 6, 256], P('scen', 'region', 'day')
- selling: float32 [4, 1600, 2, 6, 256], P('scen', 'region', 'day')
- ordering: float32 [240, 256], P('region')
- balance_dual: float32 [4, 1600, 2, 6, 256], P('scen', 'region', 'day')
- depot_dual: float32 [4, 240, 2, 256], P('scen', 'region', 'day')
The draws below stay inside these ranges and needn't reach their ends.
All inputs are finite; a program needn't handle non-finite values.
Results may differ from the reference program's by a relative error of at most 0.0003.
Values sent between devices are 32-bit elements; how exact they have to be, the bound alone decides.
No kernel may reach another device: no remote copies, remote signals or barrier semaphores. Data moves between devices by JAX's collectives and lax.ppermute only.
A program may use at most 128 MiB of HBM per device.

```python
import math
import jax
import jax.numpy as jnp
from jax import lax

SKUS = 256
STORE_REG = 100
DC_REG = 15
LANES = 128
AGES = 6
PATTERNS = 16
ITERS = 4
DAYS = 2
REGIONS = 16
SCEN = 4
STORES = 1600
DCS = 240


def touch_ends(entries, own_key, least, high):
    place = [jax.random.randint(jax.random.fold_in(own_key, axis), (), 0, length) for axis, length in enumerate(entries.shape)]
    longest = entries.shape.index(max(entries.shape))
    neighbour = place[:longest] + [(place[longest] + 1) % entries.shape[longest]] + place[longest + 1:]
    return entries.at[tuple(place)].set(least).at[tuple(neighbour)].set(high)


def block_levels(own_key, extent, split, low, largest):
    factor_of, own = 1.0, jax.random.fold_in(own_key, 6)
    for dim, blocks in split:
        draws = jnp.exp(jax.random.uniform(jax.random.fold_in(own, dim), (blocks,), jnp.float32, low / len(split), largest / len(split)))
        factor_of = factor_of * jnp.repeat(draws, extent[dim] // blocks).reshape([-1 if axis == dim else 1 for axis in range(len(extent))])
    return factor_of


def bell_draw(stream_key, shape, scale, limit, cuts=(), kind=jnp.bfloat16):
    result = scale * jax.random.normal(stream_key, shape, jnp.float32)
    if cuts:
        result = result * block_levels(stream_key, shape, cuts, -0.22, 0.18)
    return jnp.clip(result, -limit, limit).astype(kind)


def setup_inputs(seed: int = 0) -> dict:
    keys = jax.random.split(jax.random.key(seed), 23)
    return {
        "shipments_init": jnp.clip(1.0 * jax.random.uniform(keys[0], (SCEN, REGIONS, REGIONS, LANES, DAYS, SKUS), jnp.float32) ** block_levels(keys[0], (SCEN, REGIONS, REGIONS, LANES, DAYS, SKUS), ((0, 4), (1, 16), (4, 2)), -0.2, 0.2), 0.0, 1.0),
        "holdings_init": jnp.clip(2.0 * jax.random.uniform(keys[1], (SCEN, STORES, DAYS, AGES, SKUS), jnp.float32) ** block_levels(keys[1], (SCEN, STORES, DAYS, AGES, SKUS), ((0, 4), (1, 16), (2, 2)), -0.2, 0.2), 0.0, 2.0),
        "selling_init": jnp.clip(1.0 * jax.random.uniform(keys[2], (SCEN, STORES, DAYS, AGES, SKUS), jnp.float32) ** block_levels(keys[2], (SCEN, STORES, DAYS, AGES, SKUS), ((0, 4), (1, 16), (2, 2)), -0.2, 0.2), 0.0, 1.0),
        "shortage_init": jnp.clip(1.0 * jax.random.uniform(keys[3], (SCEN, STORES, DAYS, SKUS), jnp.float32) ** block_levels(keys[3], (SCEN, STORES, DAYS, SKUS), ((0, 4), (1, 16), (2, 2)), -0.2, 0.2), 0.0, 1.0),
        "ordering_init": jnp.clip(20.0 * jax.random.uniform(keys[4], (DCS, SKUS), jnp.float32) ** block_levels(keys[4], (DCS, SKUS), ((0, 16),), -0.2, 0.2), 0.0, 20.0),
        "balance_dual_init": bell_draw(keys[5], (SCEN, STORES, DAYS, AGES, SKUS), 0.5, 3.0, ((0, 4), (1, 16), (2, 2)), jnp.float32),
        "demand_dual_init": bell_draw(keys[6], (SCEN, STORES, DAYS, SKUS), 0.5, 3.0, ((0, 4), (1, 16), (2, 2)), jnp.float32),
        "depot_dual_init": jnp.clip(0.1 * jax.random.uniform(keys[7], (SCEN, DCS, DAYS, SKUS), jnp.float32) ** block_levels(keys[7], (SCEN, DCS, DAYS, SKUS), ((0, 4), (1, 16), (2, 2)), -0.2, 0.2), 0.0, 0.1),
        "demand_base": jnp.clip(jnp.exp(math.log(2.0) - 1.3862944 * jax.random.uniform(keys[8], (STORES, SKUS), jnp.float32) ** block_levels(keys[8], (STORES, SKUS), ((0, 16),), -0.2, 0.2)), 0.5, 2.0),
        "demand_pattern": jnp.clip(jnp.exp(jax.random.uniform(keys[9], (PATTERNS, SKUS), jnp.float32, math.log(0.5), math.log(2.0))), 0.5, 2.0),
        "demand_index": touch_ends(jax.random.randint(keys[10], (SCEN, STORES, DAYS), 0, PATTERNS), jax.random.fold_in(keys[10], 1), 0, PATTERNS - 1).astype(jnp.int32),
        "initial_stock": jnp.clip(2.0 * jax.random.uniform(keys[11], (STORES, AGES - 1, SKUS), jnp.float32) ** block_levels(keys[11], (STORES, AGES - 1, SKUS), ((0, 16),), -0.2, 0.2), 0.0, 2.0),
        "depot_supply": jnp.clip(jnp.exp(math.log(16.0) - 1.3862944 * jax.random.uniform(keys[12], (DCS, DAYS, SKUS), jnp.float32) ** block_levels(keys[12], (DCS, DAYS, SKUS), ((0, 16), (1, 2)), -0.2, 0.2)), 4.0, 16.0),
        "lane_cost": jnp.clip(jnp.exp(jax.random.uniform(keys[13], (REGIONS, REGIONS, LANES), jnp.float32, math.log(0.1), math.log(1.0))), 0.1, 1.0),
        "item_volume": jnp.clip(jnp.exp(jax.random.uniform(keys[14], (SKUS,), jnp.float32, math.log(0.5), math.log(2.0))), 0.5, 2.0),
        "holding_cost": jnp.clip(jnp.exp(jax.random.uniform(keys[15], (AGES, SKUS), jnp.float32, math.log(0.05), math.log(0.5))), 0.05, 0.5),
        "unit_price": jnp.clip(jnp.exp(jax.random.uniform(keys[16], (SKUS,), jnp.float32, math.log(1.0), math.log(4.0))), 1.0, 4.0),
        "short_penalty": jnp.clip(jnp.exp(jax.random.uniform(keys[17], (SKUS,), jnp.float32, math.log(2.0), math.log(8.0))), 2.0, 8.0),
        "order_cost": jnp.clip(jnp.exp(jax.random.uniform(keys[18], (SKUS,), jnp.float32, math.log(0.5), math.log(2.0))), 0.5, 2.0),
        "lane_depot": touch_ends(jax.random.randint(keys[19], (REGIONS, REGIONS, LANES), 0, DC_REG), jax.random.fold_in(keys[19], 1), 0, DC_REG - 1).astype(jnp.int32),
        "lane_store": touch_ends(jax.random.randint(keys[20], (REGIONS, REGIONS, LANES), 0, STORE_REG), jax.random.fold_in(keys[20], 1), 0, STORE_REG - 1).astype(jnp.int32),
        "lane_mask": touch_ends((jax.random.randint(keys[21], (REGIONS, REGIONS, LANES), 0, 5) < 3).astype(jnp.int32), jax.random.fold_in(keys[21], 1), 0, 1),
    }


primal_step = 0.25
order_step = 0.05
dual_step = 0.25
depot_step = 0.02


def reference(shipments_init, holdings_init, selling_init, shortage_init, ordering_init, balance_dual_init, demand_dual_init, depot_dual_init, demand_base, demand_pattern, demand_index, initial_stock, depot_supply, lane_cost, item_volume, holding_cost, unit_price, short_penalty, order_cost, lane_depot, lane_store, lane_mask):
    highest = lax.Precision.HIGHEST
    lane_weight = lane_mask.astype(jnp.float32)
    store_table = (lane_store[..., None] == jnp.arange(STORE_REG, dtype=jnp.int32)).astype(jnp.float32) * lane_weight[..., None]
    depot_table = (lane_depot[..., None] == jnp.arange(DC_REG, dtype=jnp.int32)).astype(jnp.float32) * lane_weight[..., None]
    pattern_table = (demand_index[..., None] == jnp.arange(PATTERNS, dtype=jnp.int32)).astype(jnp.float32)
    demand = jnp.einsum('nsdp,pk->nsdk', pattern_table, demand_pattern, precision=highest) * demand_base[None, :, None, :]
    lane_price = lane_cost[:, :, :, None, None] * item_volume
    keep_lanes = lane_weight[None, :, :, :, None, None]
    shipments, holdings, selling, shortage = shipments_init, holdings_init, selling_init, shortage_init
    ordering = ordering_init
    balance_dual, demand_dual, depot_dual = balance_dual_init, demand_dual_init, depot_dual_init
    for iterate in range(ITERS):
        first_age = balance_dual[:, :, :, 0, :].reshape(SCEN, REGIONS, STORE_REG, DAYS, SKUS)
        store_lanes = jnp.einsum('abls,nbstk->nabltk', store_table, first_age, precision=highest)
        depot_after = jnp.flip(jnp.cumsum(jnp.flip(depot_dual, 2), 2), 2).reshape(SCEN, REGIONS, DC_REG, DAYS, SKUS)
        depot_lanes = jnp.einsum('abld,nadtk->nabltk', depot_table, depot_after, precision=highest)
        next_dual = jnp.pad(balance_dual[:, :, 1:, 1:, :], ((0, 0), (0, 0), (0, 1), (0, 1), (0, 0)))
        new_ship = keep_lanes * jnp.maximum(0.0, shipments - primal_step * (lane_price + store_lanes + depot_lanes))
        new_hold = jnp.maximum(0.0, holdings - primal_step * (holding_cost - balance_dual + next_dual))
        new_sell = jnp.maximum(0.0, selling - primal_step * (-unit_price - balance_dual - demand_dual[:, :, :, None, :]))
        new_short = jnp.maximum(0.0, shortage - primal_step * (short_penalty - demand_dual))
        new_order = jnp.maximum(0.0, ordering - order_step * (order_cost - jnp.sum(depot_dual, axis=(0, 2))))
        ship_bar = 2.0 * new_ship - shipments
        hold_bar = 2.0 * new_hold - holdings
        sell_bar = 2.0 * new_sell - selling
        short_bar = 2.0 * new_short - shortage
        order_bar = 2.0 * new_order - ordering
        shipments, holdings, selling, shortage, ordering = new_ship, new_hold, new_sell, new_short, new_order
        arrivals = jnp.einsum('abls,nabltk->nbstk', store_table, ship_bar, precision=highest).reshape(SCEN, STORES, DAYS, SKUS)
        outflow = jnp.einsum('abld,nabltk->nadtk', depot_table, ship_bar, precision=highest).reshape(SCEN, DCS, DAYS, SKUS)
        starting = jnp.broadcast_to(initial_stock[None, :, None, :, :], (SCEN, STORES, 1, AGES - 1, SKUS))
        earlier = jnp.concatenate([starting, hold_bar[:, :, :-1, :-1, :]], axis=2)
        carried = jnp.concatenate([arrivals[:, :, :, None, :], earlier], axis=3)
        balance_dual = balance_dual - dual_step * (hold_bar + sell_bar - carried)
        demand_dual = demand_dual + dual_step * (demand - jnp.sum(sell_bar, axis=3) - short_bar)
        net_flow = outflow - depot_supply[None]
        depot_dual = jnp.maximum(0.0, depot_dual + depot_step * (jnp.cumsum(net_flow, axis=2) - order_bar[None, :, None, :]))
    return shipments, holdings, selling, ordering, balance_dual, depot_dual
```

```python
import functools

import jax
import jax.numpy as jnp
from jax import lax
from jax.experimental import pallas as pl
from jax.experimental.pallas import tpu as pltpu
from jax.sharding import PartitionSpec as P

ITERS = 4
PRIMAL_STEP = 0.25
ORDER_STEP = 0.05
DUAL_STEP = 0.25
DEPOT_STEP = 0.02

REGIONS = 16
DAYS = 2
PARTS = REGIONS * DAYS
STORES = 100
DEPOTS = 15
LANES = 128
AGES = 6
SKUS = 256
SLICE = SKUS // PARTS
PATTERNS = 16
HOLD, SELL, BAL = 0, AGES, 2 * AGES
MAIN = 3 * AGES
SHORT, DDUAL, DEMAND, STOCK = 0, 1, 2, 3
AUX = 6
OPEN = 2
SPARE = STORES
DEPOT_COLUMN = 112
DEPOT_PITCH = 16
HALF = 8

VMEM_BYTES = 56 * 1024 * 1024
f32 = jnp.float32
VM = pl.BlockSpec(memory_space=pltpu.VMEM)


def call(body, outs, count, aliases=None, cost=None):
    return pl.pallas_call(
        body,
        out_shape=outs,
        in_specs=[VM] * count,
        out_specs=jax.tree.map(lambda _: VM, outs),
        input_output_aliases=aliases or {},
        compiler_params=pltpu.CompilerParams(vmem_limit_bytes=VMEM_BYTES),
        cost_estimate=cost,
    )


def like(*shape, dtype=f32):
    return jax.ShapeDtypeStruct(shape, dtype)


def pack_ship_kernel(ship_ref, out_ref):
    def step(b, carry):
        for h in range(2):
            rows = ship_ref[pl.ds(b * (2 * LANES) + h, LANES, stride=2), :]
            out_ref[16 * h : 16 * h + 16, b] = rows.T.reshape(16, SLICE, LANES)
        return carry

    lax.fori_loop(0, REGIONS, step, 0)


def unpack_ship_kernel(in_ref, ship_ref):
    def step(b, carry):
        for h in range(2):
            cols = in_ref[16 * h : 16 * h + 16, b].reshape(LANES, LANES)
            ship_ref[pl.ds(b * (2 * LANES) + h, LANES, stride=2), :] = cols.T
        return carry

    lax.fori_loop(0, REGIONS, step, 0)


def pack_store_kernel(
    day_ref,
    hold_ref,
    sell_ref,
    bal_ref,
    short_ref,
    ddual_ref,
    base_ref,
    pattern_ref,
    index_ref,
    stock_ref,
    depot_dual_ref,
    ordering_ref,
    supply_ref,
    out_ref,
    rows,
    index,
):
    day = day_ref[0]
    rows[...] = jnp.zeros_like(rows)
    index[...] = jnp.zeros_like(index)
    index[0:1, 0:STORES] = index_ref[...]
    pick = jnp.broadcast_to(index[0:1, :], (SLICE, LANES))
    sources = ((HOLD, hold_ref), (SELL, sell_ref), (BAL, bal_ref))
    for h in range(2):
        cols = slice(h * LANES, (h + 1) * LANES)

        def put(tile, values, depots=None):
            slot = rows.at[h, tile]
            slot[0:STORES, :] = values
            if depots is not None:
                slot[SPARE : SPARE + DEPOTS, :] = depots
            out_ref[16 * h : 16 * h + 16, tile] = slot[...].T.reshape(16, SLICE, LANES)

        for first, ref in sources:
            for age in range(AGES):
                values = ref[pl.ds(2 * age + h, STORES, stride=2 * AGES), :]
                depots = None
                if first == HOLD and age == 0:
                    depots = depot_dual_ref[pl.ds(h, DEPOTS, stride=2), :]
                if first == HOLD and age == 1:
                    depots = ordering_ref[:, cols]
                if first == HOLD and age == 2:
                    depots = supply_ref[pl.ds(h, DEPOTS, stride=2), :]
                put(first + age, values, depots)
        put(MAIN + SHORT, short_ref[pl.ds(h, STORES, stride=2), :])
        put(MAIN + DDUAL, ddual_ref[pl.ds(h, STORES, stride=2), :])
        for i in range(3):
            put(
                MAIN + STOCK + i,
                jnp.where(day == 0, stock_ref[i, :, cols], stock_ref[min(i + 3, AGES - 2), :, cols]),
            )
        slot = rows.at[h, MAIN + DEMAND]
        slot[0:STORES, :] = base_ref[:, cols]
        base = slot[...].T.reshape(16, SLICE, LANES)
        slot = rows.at[h, MAIN + AUX]
        slot[0:PATTERNS, :] = pattern_ref[:, cols]
        pattern = slot[...].T.reshape(16, SLICE, LANES)
        for i in range(16):
            factor = jnp.take_along_axis(pattern[i], pick, axis=1, mode="promise_in_bounds")
            out_ref[16 * h + i, MAIN + DEMAND] = base[i] * factor


def unpack_store_kernel(in_ref, hold_ref, sell_ref, bal_ref, depot_dual_ref, ordering_ref):
    for h in range(2):
        for first, ref in ((HOLD, hold_ref), (SELL, sell_ref), (BAL, bal_ref)):
            for age in range(AGES):
                rows = in_ref[16 * h : 16 * h + 16, first + age].reshape(LANES, LANES).T
                ref[pl.ds(2 * age + h, STORES, stride=2 * AGES), :] = rows[0:STORES]
                if first == HOLD and age == 0:
                    depot_dual_ref[pl.ds(h, DEPOTS, stride=2), :] = rows[SPARE : SPARE + DEPOTS]
                if first == HOLD and age == 1:
                    ordering_ref[:, h * LANES : (h + 1) * LANES] = rows[SPARE : SPARE + DEPOTS]


def tables_kernel(store_ref, depot_ref, mask_ref, table_ref, slot_ref, weight_ref):
    column = lax.broadcasted_iota(jnp.int32, (LANES, LANES), 0)
    pitch = lax.broadcasted_iota(jnp.int32, (REGIONS, LANES), 0)

    def step(b, carry):
        for a in range(REGIONS):
            store = store_ref[a, pl.ds(b, 1), :]
            depot = depot_ref[a, pl.ds(b, 1), :] + DEPOT_COLUMN
            keep = mask_ref[a, pl.ds(b, 1), :] > 0
            store = jnp.where(keep, store, -1)
            depot = jnp.where(keep, depot, -1)
            ends = (column == store) | (column == depot)
            table_ref[a, b] = jnp.where(ends, 1.0, 0.0).astype(f32).T.astype(jnp.bfloat16)
        return carry

    lax.fori_loop(0, REGIONS, step, 0)
    for a in range(REGIONS):
        slot_ref[a] = depot_ref[a] + (a % HALF) * DEPOT_PITCH
        weight_ref[a] = mask_ref[a].astype(f32)


def lane_window(start):
    lane = lax.broadcasted_iota(jnp.int32, (SLICE, LANES), 1)
    return (lane >= start) & (lane < start + DEPOTS)


def depots_kernel(st_ref, dual_ref, ordering_ref, supply_ref, block_ref):
    for half in range(2):
        dual, supply = [], []
        ordering = jnp.zeros((SLICE, LANES), f32)
        for t in range(DAYS):
            here = jnp.zeros((SLICE, LANES), f32)
            given = jnp.zeros((SLICE, LANES), f32)
            for i in range(HALF):
                at, row = i * DEPOT_PITCH, t * REGIONS + half * HALF + i
                shift = (at - SPARE) % LANES
                window = lane_window(at)
                here = jnp.where(window, pltpu.roll(st_ref[row, HOLD], shift, 1), here)
                given = jnp.where(window, pltpu.roll(st_ref[row, HOLD + 2], shift, 1), given)
                if t == 0:
                    ordering = jnp.where(
                        window, pltpu.roll(st_ref[row, HOLD + 1], shift, 1), ordering
                    )
            dual.append(here)
            dual_ref[t, half] = here
            supply_ref[t, half] = given
        ordering_ref[half] = ordering
        block_ref[half] = dual[0] + dual[1]


def iterate_kernel(
    first,
    *refs,
):
    if first:
        ship_ref, main_ref, *refs = refs
        open_ref, fixed_ref, offset = main_ref, main_ref, MAIN
    else:
        ship_ref, main_ref, open_ref, fixed_ref, *refs = refs
        offset = 0
    skip = offset if first else -OPEN
    (
        dual_ref,
        table_ref,
        store_ref,
        slot_ref,
        cost_ref,
        weight_ref,
        vec_ref,
        ship_out,
        main_out,
        open_out,
        *fixed_out,
        flow_out,
        flow,
    ) = refs
    volume = vec_ref[0]
    price = vec_ref[1]
    penalty = vec_ref[2]
    holding_cost = [vec_ref[4 + age] for age in range(AGES)]
    flow[...] = jnp.zeros_like(flow)
    later = [
        [dual_ref[0, half] + dual_ref[1, half] for half in range(2)],
        [dual_ref[1, half] for half in range(2)],
    ]

    def step(b, carry):
        row = [b, REGIONS + b]
        bal = [[main_ref[row[t], BAL + age] for age in range(AGES)] for t in range(DAYS)]
        ended = [None, None]
        hold_bar = [[None] * AGES for _ in range(DAYS)]
        for t in range(DAYS):
            ddual = open_ref[row[t], offset + DDUAL]
            short = open_ref[row[t], offset + SHORT]
            new_short = jnp.maximum(0.0, short - PRIMAL_STEP * (penalty - ddual))
            short_bar = 2.0 * new_short - short
            open_out[row[t], SHORT] = new_short
            sold = jnp.zeros((SLICE, LANES), f32)
            for age in range(AGES):
                here = bal[t][age]
                hold = main_ref[row[t], HOLD + age]
                sell = main_ref[row[t], SELL + age]
                rise = holding_cost[age] - here
                if t == 0 and age + 1 < AGES:
                    rise = rise + bal[1][age + 1]
                new_hold = jnp.maximum(0.0, hold - PRIMAL_STEP * rise)
                new_sell = jnp.maximum(0.0, sell - PRIMAL_STEP * (-price - here - ddual))
                bar = 2.0 * new_hold - hold
                sell_bar = 2.0 * new_sell - sell
                hold_bar[t][age] = bar
                sold = sold + sell_bar
                main_out[row[t], HOLD + age] = new_hold
                main_out[row[t], SELL + age] = new_sell
                gone = bar + sell_bar
                if age == 0:
                    ended[t] = here - DUAL_STEP * gone
                else:
                    if t == 0:
                        i = age - 1
                        carried = fixed_ref[row[i // 3], skip + STOCK + i % 3]
                    else:
                        carried = hold_bar[0][age - 1]
                    main_out[row[t], BAL + age] = here - DUAL_STEP * (gone - carried)
            demand = fixed_ref[row[t], skip + DEMAND]
            open_out[row[t], DDUAL] = ddual + DUAL_STEP * (demand - sold - short_bar)
            if first:
                for i in range(AUX - OPEN):
                    fixed_out[0][row[t], i] = fixed_ref[row[t], skip + OPEN + i]
        arrived = [jnp.zeros((SLICE, LANES), f32) for _ in range(DAYS)]
        for a in range(REGIONS):
            def spread(ref):
                return jnp.broadcast_to(ref[a, pl.ds(b, 1), :], (SLICE, LANES))

            store, slot = spread(store_ref), spread(slot_ref)
            lane_price = spread(cost_ref) * volume
            weight = spread(weight_ref)
            bars = []
            for t in range(DAYS):
                ends = jnp.take_along_axis(
                    bal[t][0], store, axis=1, mode="promise_in_bounds"
                ) + jnp.take_along_axis(
                    later[t][a // HALF], slot, axis=1, mode="promise_in_bounds"
                )
                ship = ship_ref[t * REGIONS + a, b]
                new_ship = weight * jnp.maximum(0.0, ship - PRIMAL_STEP * (lane_price + ends))
                ship_out[t * REGIONS + a, b] = new_ship
                bars.append(2.0 * new_ship - ship)
            bar = jnp.concatenate(bars, axis=0)
            high = bar.astype(jnp.bfloat16)
            low = (bar - high.astype(f32)).astype(jnp.bfloat16)
            sums = jnp.dot(
                jnp.concatenate([high, low], axis=0),
                table_ref[a, b],
                preferred_element_type=f32,
            )
            sums = sums[: 2 * SLICE] + sums[2 * SLICE :]
            flow[a] = flow[a] + sums
            for t in range(DAYS):
                arrived[t] = arrived[t] + sums[t * SLICE : (t + 1) * SLICE]
        for t in range(DAYS):
            main_out[row[t], BAL] = ended[t] + DUAL_STEP * arrived[t]
        return carry

    lax.fori_loop(0, REGIONS, step, 0)
    for half in range(2):
        for t in range(DAYS):
            total = jnp.zeros((SLICE, LANES), f32)
            for i in range(HALF):
                at = i * DEPOT_PITCH
                part = flow[half * HALF + i, t * SLICE : (t + 1) * SLICE, :]
                part = pltpu.roll(part, (at - DEPOT_COLUMN) % LANES, 1)
                total = jnp.where(lane_window(at), part, total)
            flow_out[t, half] = total


def depot_step_kernel(
    last,
    dual_ref,
    ordering_ref,
    flow_ref,
    supply_ref,
    own_ref,
    near_ref,
    far_ref,
    across_ref,
    vec_ref,
    *refs,
):
    if last:
        main_ref, main_out = refs
    else:
        dual_out, ordering_out, block_out = refs
    order_cost = vec_ref[3]
    for half in range(2):
        total = (own_ref[half] + near_ref[half]) + (far_ref[half] + across_ref[half])
        old = ordering_ref[half]
        ordering = jnp.maximum(0.0, old - ORDER_STEP * (order_cost - total))
        order_bar = 2.0 * ordering - old
        net = [flow_ref[t, half] - supply_ref[t, half] for t in range(DAYS)]
        dual = [
            jnp.maximum(0.0, dual_ref[0, half] + DEPOT_STEP * (net[0] - order_bar)),
            jnp.maximum(0.0, dual_ref[1, half] + DEPOT_STEP * (net[0] + net[1] - order_bar)),
        ]
        if not last:
            ordering_out[half] = ordering
            block_out[half] = dual[0] + dual[1]
            for t in range(DAYS):
                dual_out[t, half] = dual[t]
            continue
        window = lane_window(SPARE)
        for i in range(HALF):
            shift = (SPARE - i * DEPOT_PITCH) % LANES
            orders = pltpu.roll(ordering, shift, 1)
            for t in range(DAYS):
                row = t * REGIONS + half * HALF + i
                main_out[row, HOLD] = jnp.where(
                    window, pltpu.roll(dual[t], shift, 1), main_ref[row, HOLD]
                )
                main_out[row, HOLD + 1] = jnp.where(window, orders, main_ref[row, HOLD + 1])


def swap(parts):
    return lax.all_to_all(parts, ("day", "region"), 0, 0, tiled=True)


def scenario_blocks(block):
    def partner(bit):
        return lax.ppermute(block, "scen", [(n, n ^ bit) for n in range(4)])

    return block, partner(1), partner(2), partner(3)


def per_device(
    shipments_init,
    holdings_init,
    selling_init,
    shortage_init,
    ordering_init,
    balance_dual_init,
    demand_dual_init,
    depot_dual_init,
    demand_base,
    demand_pattern,
    demand_index,
    initial_stock,
    depot_supply,
    lane_cost,
    item_volume,
    holding_cost,
    unit_price,
    short_penalty,
    order_cost,
    lane_depot,
    lane_store,
    lane_mask,
):
    day = lax.axis_index("day").astype(jnp.int32)
    part = day * REGIONS + lax.axis_index("region")
    tile = (PARTS, AUX + MAIN, SLICE, LANES)
    packed = pl.pallas_call(
        pack_store_kernel,
        out_shape=like(*tile),
        in_specs=[pl.BlockSpec(memory_space=pltpu.SMEM)] + [VM] * 12,
        out_specs=VM,
        scratch_shapes=[
            pltpu.VMEM((2, MAIN + AUX + 1, LANES, LANES), f32),
            pltpu.VMEM((SLICE, LANES), jnp.int32),
        ],
        compiler_params=pltpu.CompilerParams(vmem_limit_bytes=VMEM_BYTES),
    )(
        day.reshape(1),
        holdings_init.reshape(-1, LANES),
        selling_init.reshape(-1, LANES),
        balance_dual_init.reshape(-1, LANES),
        shortage_init.reshape(-1, LANES),
        demand_dual_init.reshape(-1, LANES),
        demand_base,
        demand_pattern,
        demand_index.reshape(1, STORES),
        jnp.transpose(initial_stock, (1, 0, 2)),
        depot_dual_init.reshape(-1, LANES),
        ordering_init,
        depot_supply.reshape(-1, LANES),
    )
    stores = swap(packed)
    ship = call(pack_ship_kernel, like(PARTS, REGIONS, SLICE, LANES), 1)(
        shipments_init.reshape(-1, LANES)
    )
    ship = swap(ship)
    table, slot, weight = call(
        tables_kernel,
        (
            like(REGIONS, REGIONS, LANES, LANES, dtype=jnp.bfloat16),
            like(REGIONS, REGIONS, LANES, dtype=jnp.int32),
            like(REGIONS, REGIONS, LANES),
        ),
        3,
    )(lane_store, lane_depot, lane_mask)
    vectors = jnp.concatenate(
        [jnp.stack([item_volume, unit_price, short_penalty, order_cost]), holding_cost], axis=0
    )
    vectors = lax.dynamic_slice(vectors, (0, part * SLICE), (vectors.shape[0], SLICE))
    vectors = jnp.broadcast_to(vectors[:, :, None], (*vectors.shape, LANES))
    depots = like(DAYS, 2, SLICE, LANES)
    one_day = like(2, SLICE, LANES)
    dual, ordering, supply, block = call(
        depots_kernel, (depots, one_day, depots, one_day), 1
    )(stores)
    main = opened = fixed = None
    for iteration in range(ITERS):
        blocks = scenario_blocks(block)
        first = iteration == 0
        state = (ship, stores) if first else (ship, main, opened, fixed)
        outs = (
            like(PARTS, REGIONS, SLICE, LANES),
            like(PARTS, MAIN, SLICE, LANES),
            like(PARTS, OPEN, SLICE, LANES),
            *([like(PARTS, AUX - OPEN, SLICE, LANES)] if first else []),
            depots,
        )
        ship, main, opened, *keep, flow = pl.pallas_call(
            functools.partial(iterate_kernel, first),
            out_shape=outs,
            in_specs=[VM] * (len(state) + 7),
            out_specs=(VM,) * len(outs),
            scratch_shapes=[pltpu.VMEM((REGIONS, 2 * SLICE, LANES), f32)],
            input_output_aliases={0: 0} if first else {0: 0, 1: 1, 2: 2},
            compiler_params=pltpu.CompilerParams(vmem_limit_bytes=VMEM_BYTES),
        )(*state, dual, table, lane_store, slot, lane_cost, weight, vectors)
        if first:
            (fixed,) = keep
        last = iteration == ITERS - 1
        operands = (dual, ordering, flow, supply, *blocks, vectors)
        if last:
            spare = pl.BlockSpec((PARTS, 2, SLICE, LANES), lambda i: (0, 0, 0, 0))
            main = pl.pallas_call(
                functools.partial(depot_step_kernel, True),
                grid=(1,),
                out_shape=like(PARTS, MAIN, SLICE, LANES),
                in_specs=[VM] * len(operands) + [spare],
                out_specs=spare,
                input_output_aliases={len(operands): 0},
                compiler_params=pltpu.CompilerParams(vmem_limit_bytes=VMEM_BYTES),
            )(*operands, main)
        else:
            dual, ordering, block = call(
                functools.partial(depot_step_kernel, False),
                (depots, one_day, one_day),
                len(operands),
            )(*operands)
    ship = swap(ship)
    main = swap(main)
    shipments = call(unpack_ship_kernel, like(2 * REGIONS * LANES, LANES), 1)(ship)
    flat = like(STORES * 2 * AGES, LANES)
    holdings, selling, balance, depot_dual, ordering = call(
        unpack_store_kernel,
        (flat, flat, flat, like(2 * DEPOTS, LANES), like(DEPOTS, SKUS)),
        1,
    )(main)
    return (
        shipments.reshape(1, 1, REGIONS, LANES, 1, SKUS),
        holdings.reshape(1, STORES, 1, AGES, SKUS),
        selling.reshape(1, STORES, 1, AGES, SKUS),
        ordering,
        balance.reshape(1, STORES, 1, AGES, SKUS),
        depot_dual.reshape(1, DEPOTS, 1, SKUS),
    )


def solution(mesh):
    placed = (
        P("scen", "region", None, None, "day", None),
        P("scen", "region", "day", None, None),
        P("scen", "region", "day", None, None),
        P("scen", "region", "day", None),
        P("region", None),
        P("scen", "region", "day", None, None),
        P("scen", "region", "day", None),
        P("scen", "region", "day", None),
        P("region", None),
        P(),
        P("scen", "region", "day"),
        P("region", None, None),
        P("region", "day", None),
        P(),
        P(),
        P(),
        P(),
        P(),
        P(),
        P(),
        P(),
        P(),
    )
    return jax.shard_map(
        per_device,
        mesh=mesh,
        in_specs=placed,
        out_specs=(
            P("scen", "region", None, None, "day", None),
            P("scen", "region", "day", None, None),
            P("scen", "region", "day", None, None),
            P("region", None),
            P("scen", "region", "day", None, None),
            P("scen", "region", "day", None),
        ),
        check_vma=False,
    )
```

```python
import functools

import jax
import jax.numpy as jnp
from jax import lax
from jax.experimental import pallas as pl
from jax.experimental.pallas import tpu as pltpu
from jax.sharding import PartitionSpec as P

ITERS = 4
PRIMAL_STEP = 0.25
ORDER_STEP = 0.05
DUAL_STEP = 0.25
DEPOT_STEP = 0.02

REGIONS = 16
PAIRS = REGIONS // 2
DAYS = 2
PARTS = REGIONS * DAYS
STORES = 100
QUARTER = STORES // 4
DEPOTS = 15
LANES = 128
AGES = 6
SKUS = 256
SCENARIOS = 4
HALVES = 2
SLICE = SKUS // HALVES // PARTS
ROWS = 2 * SLICE
HOLD, SELL, BAL, STOCK = 0, 3, 6, 9
MAIN = 9
TILES = 10
OUT_TILES = 8
SPARE = STORES
DEPOT_COLUMN = 112
DEPOT_PITCH = 16
GROUP = 8

VMEM_BYTES = 16 * 1024 * 1024
f32 = jnp.float32
VM = pl.BlockSpec(memory_space=pltpu.VMEM)
SM = pl.BlockSpec(memory_space=pltpu.SMEM)
HB = pl.BlockSpec(memory_space=pltpu.HBM)


def call(body, outs, specs, aliases=None, scratch=(), micros=1, out_specs=None):
    return pl.pallas_call(
        body,
        out_shape=outs,
        in_specs=[VM] * specs if isinstance(specs, int) else specs,
        out_specs=jax.tree.map(lambda _: VM, outs) if out_specs is None else out_specs,
        scratch_shapes=list(scratch),
        input_output_aliases=aliases or {},
        compiler_params=pltpu.CompilerParams(vmem_limit_bytes=VMEM_BYTES),
        cost_estimate=pl.CostEstimate(
            flops=micros * 500_000_000, bytes_accessed=micros * 3_000_000, transcendentals=0
        ),
    )


def like(*shape, dtype=f32):
    return jax.ShapeDtypeStruct(shape, dtype)


def near(*shape, dtype=f32):
    return pltpu.VMEM(shape, dtype)


def turn(x):
    return pltpu.roll(x, SLICE, x.ndim - 2)


def low_rows(shape):
    return lax.broadcasted_iota(jnp.int32, shape, len(shape) - 2) % ROWS < SLICE


def lane_window(start, size):
    lane = lax.broadcasted_iota(jnp.int32, (ROWS, LANES), 1)
    return (lane >= start) & (lane < start + size)


def pack_kernel(half, day_ref, *refs):
    given, out_ref, held = refs[:13], refs[13], refs[14:27]
    packed, rows, index, came, left = refs[27:]
    (
        ship_ref,
        hold_ref,
        sell_ref,
        bal_ref,
        short_ref,
        ddual_ref,
        base_ref,
        pattern_ref,
        index_ref,
        stock_ref,
        depot_dual_ref,
        ordering_ref,
        supply_ref,
    ) = held
    coming = [pltpu.make_async_copy(given[i], held[i], came.at[i]) for i in range(13)]
    for copy in coming:
        copy.start()
    day = day_ref[0]
    cols = slice(half * LANES, (half + 1) * LANES)
    low = low_rows((16, ROWS, LANES))

    def put(tile, first, second):
        first = first.T.reshape(16, ROWS, LANES)
        second = second.T.reshape(16, ROWS, LANES)
        packed[:, 0, tile] = jnp.where(low, first, turn(second))
        packed[:, 1, tile] = jnp.where(low, turn(first), second)

    def ship_step(pair, carry):
        at = pair * (4 * LANES) + half
        put(
            TILES + pair,
            ship_ref[pl.ds(at, LANES, stride=2), :],
            ship_ref[pl.ds(at + 2 * LANES, LANES, stride=2), :],
        )
        return carry

    coming[0].wait()
    lax.fori_loop(0, PAIRS, ship_step, 0)
    going = [
        pltpu.make_async_copy(
            packed.at[:, :, pl.ds(first, size)], out_ref.at[:, :, pl.ds(first, size)], left.at[i]
        )
        for i, (first, size) in enumerate(((0, TILES), (TILES, PAIRS)))
    ]
    going[1].start()
    for copy in coming[1:]:
        copy.wait()

    index[...] = jnp.zeros_like(index)
    index[0:1, 0:STORES] = index_ref[...]
    patterns = pattern_ref.shape[0]
    chosen = lax.broadcasted_iota(jnp.int32, (patterns, LANES), 0) == index[0:1, :]
    factor = lax.dot_general(
        chosen.astype(f32),
        pattern_ref[:, cols],
        (((0,), (0,)), ((), ())),
        precision=lax.Precision.HIGHEST,
        preferred_element_type=f32,
    )
    demand = factor[0:STORES] * base_ref[:, cols]
    for tile in range(TILES):
        for side in range(2):
            slot = rows.at[2 * tile + side]
            slot[96:LANES, :] = jnp.zeros((LANES - 96, LANES), f32)
            if tile < MAIN:
                ref = (hold_ref, sell_ref, bal_ref)[tile // 3]
                age = 2 * (tile % 3) + side
                slot[0:STORES, :] = ref[pl.ds(2 * age + half, STORES, stride=2 * AGES), :]
            else:
                slot[0:STORES, :] = stock_ref[1 + side + 2 * day, :, cols]
            quarter = QUARTER * (tile % 4)
            if tile < 4:
                ref = (short_ref, ddual_ref)[side]
                slot[SPARE : SPARE + QUARTER, :] = ref[
                    pl.ds(2 * quarter + half, QUARTER, stride=2), :
                ]
            elif tile < 8:
                given = demand if side == 0 else stock_ref[0, :, cols]
                slot[SPARE : SPARE + QUARTER, :] = given[quarter : quarter + QUARTER]
            elif tile == 8:
                given = depot_dual_ref[:, 0, cols] if side == 0 else ordering_ref[:, cols]
                slot[SPARE : SPARE + DEPOTS, :] = given
            elif side == 0:
                slot[SPARE : SPARE + DEPOTS, :] = supply_ref[:, 0, cols]
        put(tile, rows[2 * tile], rows[2 * tile + 1])
    going[0].start()
    for copy in going:
        copy.wait()


def unpack_kernel(half, in_ref, *refs):
    earlier = refs[: 6 * half]
    outs = refs[6 * half : 6 * half + 6]
    *held, left = refs[6 * half + 6 :]
    ship_ref, hold_ref, sell_ref, bal_ref, depot_dual_ref, ordering_ref = held
    going = [pltpu.make_async_copy(held[i], outs[i], left.at[i]) for i in range(6)]
    low = low_rows((16, ROWS, LANES))
    pace = half + 1

    def get(tile):
        lower, upper = in_ref[:, 0, tile], in_ref[:, 1, tile]
        first = jnp.where(low, lower, turn(upper))
        second = jnp.where(low, turn(lower), upper)
        return first.reshape(LANES, LANES).T, second.reshape(LANES, LANES).T

    def ship_step(pair, carry):
        at = pair * (2 * LANES * pace) + half
        first, second = get(OUT_TILES + pair)
        ship_ref[pl.ds(at, LANES, stride=pace), :] = first
        ship_ref[pl.ds(at + LANES * pace, LANES, stride=pace), :] = second
        if half:
            span = 2 * LANES
            ship_ref[pl.ds(2 * span * pair, span, stride=2), :] = earlier[0][
                pl.ds(span * pair, span), :
            ]
        return carry

    lax.fori_loop(0, PAIRS, ship_step, 0)
    going[0].start()
    if half:
        for i, ref in ((1, hold_ref), (2, sell_ref), (3, bal_ref)):
            ref[pl.ds(0, STORES * AGES, stride=2), :] = earlier[i][...]
        depot_dual_ref[:, 0, :LANES] = earlier[4][...]
        ordering_ref[:, :LANES] = earlier[5][...]
    for tile in range(OUT_TILES):
        both = get(tile)
        ref = (hold_ref, sell_ref, bal_ref)[tile // 3]
        for side in range(2):
            age = 2 * (tile % 3) + side
            ref[pl.ds(pace * age + half, STORES, stride=pace * AGES), :] = both[side][0:STORES]
            if tile < 4:
                at = pace * (AGES * QUARTER * tile + 4 + side) + half
                bal_ref[pl.ds(at, QUARTER, stride=pace * AGES), :] = both[side][
                    SPARE : SPARE + QUARTER
                ]
        if tile == 4:
            depots = [rows[SPARE : SPARE + DEPOTS] for rows in both]
            if half:
                depot_dual_ref[:, 0, LANES:] = depots[0]
                ordering_ref[:, LANES:] = depots[1]
            else:
                depot_dual_ref[...] = depots[0]
                ordering_ref[...] = depots[1]
    for copy in going[1:]:
        copy.start()
    for copy in going:
        copy.wait()


def tables_kernel(
    day_ref,
    store_ref,
    depot_ref,
    mask_ref,
    cost_ref,
    table_ref,
    near_store,
    near_slot,
    near_cost,
    near_keep,
    next_ref,
):
    next_ref[0] = day_ref[0]
    column = lax.broadcasted_iota(jnp.int32, (LANES, LANES), 0)
    low = low_rows((ROWS, LANES))

    def step(pair, carry):
        for a in range(REGIONS):
            def spread(ref):
                return jnp.where(
                    low,
                    jnp.broadcast_to(ref[a, pl.ds(2 * pair, 1), :], (ROWS, LANES)),
                    jnp.broadcast_to(ref[a, pl.ds(2 * pair + 1, 1), :], (ROWS, LANES)),
                )

            near_store[a, pair] = spread(store_ref)
            near_slot[a, pair] = spread(depot_ref) + (a % GROUP) * DEPOT_PITCH
            near_cost[a, pair] = spread(cost_ref)
            near_keep[a, pair] = spread(mask_ref).astype(f32)
            for side in range(2):
                b = 2 * pair + side
                store = store_ref[a, pl.ds(b, 1), :]
                depot = depot_ref[a, pl.ds(b, 1), :] + DEPOT_COLUMN
                keep = mask_ref[a, pl.ds(b, 1), :] > 0
                store = jnp.where(keep, store, -1)
                depot = jnp.where(keep, depot, -1)
                ends = (column == store) | (column == depot)
                table_ref[pair, a, :, side * LANES : (side + 1) * LANES] = (
                    jnp.where(ends, 1.0, 0.0).astype(f32).T.astype(jnp.bfloat16)
                )
        return carry

    lax.fori_loop(0, PAIRS, step, 0)


def unfold_kernel(
    in_ref, open_ref, fixed_ref, stock_ref, dual_ref, ordering_ref, supply_ref, block_ref
):
    low = low_rows((ROWS, LANES))
    windows = [lane_window(QUARTER * q, QUARTER) for q in range(4)]

    def step(row, carry):
        stock_ref[row] = in_ref[row, STOCK]
        for first, ref in ((0, open_ref), (4, fixed_ref)):
            total = jnp.zeros((ROWS, LANES), f32)
            for q in range(4):
                part = pltpu.roll(in_ref[row, first + q], (QUARTER * q - SPARE) % LANES, 1)
                total = jnp.where(windows[q], part, total)
            ref[row] = total
        return carry

    lax.fori_loop(0, PARTS, step, 0)
    for group in range(2):
        dual = []
        for t in range(DAYS):
            here = jnp.zeros((ROWS, LANES), f32)
            given = jnp.zeros((ROWS, LANES), f32)
            for i in range(GROUP):
                at, row = i * DEPOT_PITCH, t * REGIONS + group * GROUP + i
                shift = (at - SPARE) % LANES
                window = lane_window(at, DEPOTS)
                here = jnp.where(window, pltpu.roll(in_ref[row, 8], shift, 1), here)
                given = jnp.where(window, pltpu.roll(in_ref[row, 9], shift, 1), given)
            dual.append(jnp.where(low, here, turn(here)))
            dual_ref[t, group] = dual[t]
            supply_ref[t, group] = jnp.where(low, given, turn(given))
            if t == 0:
                ordering_ref[group] = jnp.where(low, turn(here), here)
        block_ref[group] = dual[0] + dual[1]


def iterate_kernel(first, part, *refs):
    if first:
        main_ref, *refs = refs
        ship_ref, ship_tile = main_ref, TILES
        if part == 1:
            refs = refs[2:]
        open_ref, *refs = refs
    else:
        ship_ref, main_ref, open_ref, *refs = refs
        ship_tile = 0
    if part == 1:
        flow_ref, *refs = refs
    (
        fixed_ref,
        stock_ref,
        dual_ref,
        table_ref,
        store_ref,
        slot_ref,
        cost_ref,
        keep_ref,
        vec_ref,
        ship_out,
        main_out,
        open_out,
        flow_out,
    ) = refs[:13]
    volume, price, penalty = (vec_ref[i] for i in range(3))
    holding_cost = [vec_ref[4 + p] for p in range(3)]
    low = low_rows((ROWS, LANES))
    low_days = low_rows((DAYS * ROWS, LANES))
    flow = flow_out if part == 0 else refs[13]
    flow[...] = jnp.zeros_like(flow) if part == 0 else flow_ref[...]
    later = [
        [dual_ref[0, group] + dual_ref[1, group] for group in range(2)],
        [dual_ref[1, group] for group in range(2)],
    ]

    def store_step(b):
        row = [b, REGIONS + b]
        bal = [[main_ref[row[t], BAL + p] for p in range(3)] for t in range(DAYS)]
        before, ended = None, []
        for t in range(DAYS):
            opened, fixed = open_ref[row[t]], fixed_ref[row[t]]
            ddual = jnp.where(low, turn(opened), opened)
            new_short = jnp.maximum(0.0, opened - PRIMAL_STEP * (penalty - ddual))
            short_bar = 2.0 * new_short - opened
            sold = jnp.zeros((ROWS, LANES), f32)
            bars, gone = [], []
            for p in range(3):
                hold, sell = main_ref[row[t], HOLD + p], main_ref[row[t], SELL + p]
                rise = holding_cost[p] - bal[t][p]
                if t == 0:
                    after = turn(bal[1][p + 1]) if p < 2 else 0.0
                    rise = rise + jnp.where(low, turn(bal[1][p]), after)
                new_hold = jnp.maximum(0.0, hold - PRIMAL_STEP * rise)
                new_sell = jnp.maximum(0.0, sell - PRIMAL_STEP * (-price - bal[t][p] - ddual))
                main_out[row[t], HOLD + p] = new_hold
                main_out[row[t], SELL + p] = new_sell
                bars.append(2.0 * new_hold - hold)
                sell_bar = 2.0 * new_sell - sell
                sold = sold + sell_bar
                gone.append(bars[p] + sell_bar)
            sold = sold + turn(sold)
            wanted = turn(fixed - short_bar)
            open_out[row[t]] = jnp.where(low, new_short, opened + DUAL_STEP * (wanted - sold))
            if t == 0:
                carried = [jnp.where(low, 0.0, fixed), stock_ref[row[0]], stock_ref[row[1]]]
            else:
                carried = [
                    jnp.where(low, turn(before[p - 1]) if p else 0.0, turn(before[p]))
                    for p in range(3)
                ]
            before = bars
            for p in range(1, 3):
                main_out[row[t], BAL + p] = bal[t][p] - DUAL_STEP * (gone[p] - carried[p])
            ended.append(bal[t][0] - DUAL_STEP * (gone[0] - carried[0]))
        return row, [bal[t][0] for t in range(DAYS)], ended

    def step(pair, carry):
        row0, price0, ended0 = store_step(2 * pair)
        row1, price1, ended1 = store_step(2 * pair + 1)
        prices = [jnp.where(low, price0[t], turn(price1[t])) for t in range(DAYS)]
        arrived = jnp.zeros((DAYS * ROWS, LANES), f32)
        for a in range(REGIONS):
            store, slot = store_ref[a, pair], slot_ref[a, pair]
            lane_price = cost_ref[a, pair] * volume
            keep = keep_ref[a, pair]
            bars = []
            for t in range(DAYS):
                ends = jnp.take_along_axis(
                    prices[t], store, axis=1, mode="promise_in_bounds"
                ) + jnp.take_along_axis(
                    later[t][a // GROUP], slot, axis=1, mode="promise_in_bounds"
                )
                ship = ship_ref[t * REGIONS + a, ship_tile + pair]
                new_ship = keep * jnp.maximum(0.0, ship - PRIMAL_STEP * (lane_price + ends))
                ship_out[t * REGIONS + a, pair] = new_ship
                bars.append(2.0 * new_ship - ship)
            bar = jnp.concatenate(bars, axis=0)
            high = bar.astype(jnp.bfloat16)
            rest = (bar - high.astype(f32)).astype(jnp.bfloat16)
            sums = jnp.dot(
                jnp.concatenate([high, rest], axis=0),
                table_ref[pair, a],
                preferred_element_type=f32,
            )
            sums = sums[: DAYS * ROWS] + sums[DAYS * ROWS :]
            sums = jnp.where(low_days, sums[:, :LANES], sums[:, LANES:])
            flow[a] = flow[a] + sums
            arrived = arrived + sums
        for t in range(DAYS):
            here = arrived[t * ROWS : (t + 1) * ROWS]
            main_out[row0[t], BAL] = ended0[t] + DUAL_STEP * jnp.where(low, here, 0.0)
            main_out[row1[t], BAL] = ended1[t] + DUAL_STEP * jnp.where(low, turn(here), 0.0)
        return carry

    lax.fori_loop(part * PAIRS // 2, (part + 1) * PAIRS // 2, step, 0)
    if part == 0:
        return
    for group in range(2):
        for t in range(DAYS):
            total = jnp.zeros((ROWS, LANES), f32)
            for i in range(GROUP):
                at = i * DEPOT_PITCH
                piece = flow[group * GROUP + i, t * ROWS : (t + 1) * ROWS, :]
                piece = pltpu.roll(piece + turn(piece), (at - DEPOT_COLUMN) % LANES, 1)
                total = jnp.where(lane_window(at, DEPOTS), piece, total)
            flow_out[t, group] = total


def depot_step_kernel(
    last, dual_ref, ordering_ref, flow_ref, supply_ref, own_ref, other_ref, vec_ref, *refs
):
    order_cost = vec_ref[3]
    low = low_rows((ROWS, LANES))
    if last:
        ship_ref, main_ref, out_ref, mixed_ref, left = refs
        going = [
            pltpu.make_async_copy(
                ship_ref, out_ref.at[:, pl.ds(OUT_TILES, PAIRS)], left.at[0]
            ),
            pltpu.make_async_copy(
                main_ref.at[:, pl.ds(5, OUT_TILES - 5)],
                out_ref.at[:, pl.ds(5, OUT_TILES - 5)],
                left.at[1],
            ),
            pltpu.make_async_copy(mixed_ref, out_ref.at[:, pl.ds(0, 5)], left.at[2]),
        ]
        going[0].start()
        going[1].start()

        def step(row, carry):
            hosted = main_ref[row, OUT_TILES]
            for tile in range(4):
                shift = (SPARE - QUARTER * tile) % LANES
                mixed_ref[row, tile] = jnp.where(
                    lane_window(SPARE, QUARTER), pltpu.roll(hosted, shift, 1), main_ref[row, tile]
                )
            return carry

        lax.fori_loop(0, PARTS, step, 0)
    else:
        dual_out, ordering_out, block_out = refs
    for group in range(2):
        total = own_ref[group] + other_ref[group]
        old = ordering_ref[group]
        ordering = jnp.maximum(0.0, old - ORDER_STEP * (order_cost - total))
        order_bar = 2.0 * ordering - old
        net = [flow_ref[t, group] - supply_ref[t, group] for t in range(DAYS)]
        dual = [
            jnp.maximum(0.0, dual_ref[0, group] + DEPOT_STEP * (net[0] - order_bar)),
            jnp.maximum(0.0, dual_ref[1, group] + DEPOT_STEP * (net[0] + net[1] - order_bar)),
        ]
        if not last:
            ordering_out[group] = ordering
            block_out[group] = dual[0] + dual[1]
            for t in range(DAYS):
                dual_out[t, group] = dual[t]
            continue
        for i in range(GROUP):
            shift = (SPARE - i * DEPOT_PITCH) % LANES
            for t in range(DAYS):
                row = t * REGIONS + group * GROUP + i
                mixed = jnp.where(low, dual[t], ordering)
                mixed_ref[row, 4] = jnp.where(
                    lane_window(SPARE, DEPOTS), pltpu.roll(mixed, shift, 1), main_ref[row, 4]
                )
    if last:
        going[2].start()
        for copy in going:
            copy.wait()


def swap(parts):
    flat = parts.reshape(PARTS, -1, ROWS, LANES)
    return lax.all_to_all(flat, ("day", "region"), 0, 0, tiled=True)


def partner(block, bit):
    return lax.ppermute(block, "scen", [(n, n ^ bit) for n in range(SCENARIOS)])


def iterations(arrived, tables, vectors):
    depots = (DAYS, 2, ROWS, LANES)
    one_day = (2, ROWS, LANES)
    state = (PARTS, PAIRS, ROWS, LANES), (PARTS, MAIN, ROWS, LANES), (PARTS, ROWS, LANES)
    opened, fixed, stock, dual, ordering, supply, block = call(
        unfold_kernel,
        (
            near(*state[2]),
            near(*state[2]),
            near(*state[2]),
            like(*depots),
            like(*one_day),
            like(*depots),
            like(*one_day),
        ),
        1,
        micros=3,
    )(arrived)
    states = tuple(near(*shape) for shape in state)
    ship = main = None
    for iteration in range(ITERS):
        first = iteration == 0
        fixed_operands = (fixed, stock, dual, *tables, vectors)
        beside = partner(block, 1)
        operands = (arrived, opened) if first else (ship, main, opened)
        ship, main, opened, flow = call(
            functools.partial(iterate_kernel, first, 0),
            (*states, near(REGIONS, DAYS * ROWS, LANES)),
            len(operands) + len(fixed_operands),
            {1: 2} if first else {0: 0, 1: 1, 2: 2},
            micros=3,
        )(*operands, *fixed_operands)
        block = block + beside
        across = partner(block, SCENARIOS - 1)
        operands = (arrived, ship, main, opened) if first else (ship, main, opened)
        ship, main, opened, flow = call(
            functools.partial(iterate_kernel, first, 1),
            (*states, like(*depots)),
            1 + len(operands) + len(fixed_operands),
            {first + i: i for i in range(3)},
            scratch=[pltpu.VMEM((REGIONS, DAYS * ROWS, LANES), f32)],
            micros=3,
        )(*operands, flow, *fixed_operands)
        operands = (dual, ordering, flow, supply, block, across, vectors)
        if iteration < ITERS - 1:
            dual, ordering, block = call(
                functools.partial(depot_step_kernel, False),
                (like(*depots), like(*one_day), like(*one_day)),
                len(operands),
            )(*operands)
    return call(
        functools.partial(depot_step_kernel, True),
        pltpu.HBM((PARTS, OUT_TILES + PAIRS, ROWS, LANES), f32),
        len(operands) + 2,
        scratch=[pltpu.VMEM((PARTS, 5, ROWS, LANES), f32), pltpu.SemaphoreType.DMA((3,))],
        micros=2,
        out_specs=HB,
    )(*operands, ship, main)


def per_device(
    shipments_init,
    holdings_init,
    selling_init,
    shortage_init,
    ordering_init,
    balance_dual_init,
    demand_dual_init,
    depot_dual_init,
    demand_base,
    demand_pattern,
    demand_index,
    initial_stock,
    depot_supply,
    lane_cost,
    item_volume,
    holding_cost,
    unit_price,
    short_penalty,
    order_cost,
    lane_depot,
    lane_store,
    lane_mask,
):
    day = lax.axis_index("day").astype(jnp.int32)
    part = day * REGIONS + lax.axis_index("region")
    given = (
        shipments_init.reshape(-1, LANES),
        holdings_init.reshape(-1, LANES),
        selling_init.reshape(-1, LANES),
        balance_dual_init.reshape(-1, LANES),
        shortage_init.reshape(-1, LANES),
        demand_dual_init.reshape(-1, LANES),
        demand_base,
        demand_pattern,
        demand_index.reshape(1, STORES),
        jnp.transpose(initial_stock, (1, 0, 2)),
        depot_dual_init.reshape(DEPOTS, 1, SKUS),
        ordering_init,
        depot_supply,
    )
    day = day.reshape(1)
    arrived, tables = [], ()
    for half in range(HALVES):
        packed = call(
            functools.partial(pack_kernel, half),
            pltpu.HBM((PARTS // 2, 2, TILES + PAIRS, ROWS, LANES), f32),
            [SM] + [HB] * len(given),
            scratch=[
                *(pltpu.VMEM(array.shape, array.dtype) for array in given),
                pltpu.VMEM((PARTS // 2, 2, TILES + PAIRS, ROWS, LANES), f32),
                pltpu.VMEM((2 * TILES, LANES, LANES), f32),
                pltpu.VMEM((8, LANES), jnp.int32),
                pltpu.SemaphoreType.DMA((len(given),)),
                pltpu.SemaphoreType.DMA((2,)),
            ],
            micros=4,
            out_specs=HB,
        )(day, *given)
        arrived.append(swap(packed))
        if half == 0:
            rows = (REGIONS, PAIRS, ROWS, LANES)
            *tables, day = call(
                tables_kernel,
                (
                    near(PAIRS, REGIONS, LANES, 2 * LANES, dtype=jnp.bfloat16),
                    near(*rows, dtype=jnp.int32),
                    near(*rows, dtype=jnp.int32),
                    near(*rows),
                    near(*rows),
                    like(1, dtype=jnp.int32),
                ),
                [SM] + [VM] * 4,
                micros=5,
                out_specs=(VM,) * 5 + (SM,),
            )(day, lane_store, lane_depot, lane_mask, lane_cost)
    plain = jnp.stack([item_volume, unit_price, short_penalty, order_cost])
    vectors = []
    for half in range(HALVES):
        at = half * (SKUS // HALVES) + part * SLICE
        once = lax.dynamic_slice(plain, (0, at), (4, SLICE))
        ages = lax.dynamic_slice(holding_cost, (0, at), (AGES, SLICE))
        both = jnp.concatenate(
            [jnp.concatenate([once, once], axis=1), ages.reshape(AGES // 2, ROWS)], axis=0
        )
        vectors.append(jnp.broadcast_to(both[:, :, None], (*both.shape, LANES)))
    back = [swap(iterations(arrived[h], tables, vectors[h])) for h in range(HALVES)]
    done = ()
    for half in range(HALVES):
        pace = half + 1
        flat = (STORES * pace * AGES, LANES)
        shapes = (
            (pace * REGIONS * LANES, LANES),
            flat,
            flat,
            flat,
            (DEPOTS, 1, SKUS) if half else (DEPOTS, LANES),
            (DEPOTS, pace * LANES),
        )
        done = call(
            functools.partial(unpack_kernel, half),
            tuple(pltpu.HBM(shape, f32) for shape in shapes),
            1 + len(done),
            scratch=[
                *(pltpu.VMEM(shape, f32) for shape in shapes),
                pltpu.SemaphoreType.DMA((len(shapes),)),
            ],
            micros=4,
            out_specs=(HB,) * len(shapes),
        )(back[half].reshape(PARTS // 2, 2, -1, ROWS, LANES), *done)
    shipments, holdings, selling, balance, depot_dual, ordering = done
    return (
        shipments.reshape(1, 1, REGIONS, LANES, 1, SKUS),
        holdings.reshape(1, STORES, 1, AGES, SKUS),
        selling.reshape(1, STORES, 1, AGES, SKUS),
        ordering,
        balance.reshape(1, STORES, 1, AGES, SKUS),
        depot_dual.reshape(1, DEPOTS, 1, SKUS),
    )


def solution(mesh):
    placed = (
        P("scen", "region", None, None, "day", None),
        P("scen", "region", "day", None, None),
        P("scen", "region", "day", None, None),
        P("scen", "region", "day", None),
        P("region", None),
        P("scen", "region", "day", None, None),
        P("scen", "region", "day", None),
        P("scen", "region", "day", None),
        P("region", None),
        P(),
        P("scen", "region", "day"),
        P("region", None, None),
        P("region", "day", None),
        P(),
        P(),
        P(),
        P(),
        P(),
        P(),
        P(),
        P(),
        P(),
    )
    return jax.shard_map(
        per_device,
        mesh=mesh,
        in_specs=placed,
        out_specs=(
            P("scen", "region", None, None, "day", None),
            P("scen", "region", "day", None, None),
            P("scen", "region", "day", None, None),
            P("region", None),
            P("scen", "region", "day", None, None),
            P("scen", "region", "day", None),
        ),
        check_vma=False,
    )
```

```python
import functools

import jax
import jax.numpy as jnp
from jax import lax
from jax.experimental import pallas as pl
from jax.experimental.pallas import tpu as pltpu
from jax.sharding import PartitionSpec as P

ITERS = 4
PRIMAL_STEP = 0.25
ORDER_STEP = 0.05
DUAL_STEP = 0.25
DEPOT_STEP = 0.02

REGIONS = 16
DAYS = 2
SCENARIOS = 4
ROWS = DAYS * SCENARIOS
PARTS = REGIONS * ROWS
STORES = 100
QUARTER = STORES // 4
DEPOTS = 15
LANES = 128
AGES = 6
SKUS = 256
HALVES = 2
HOLD, SELL, BAL = 0, AGES, 2 * AGES
MAIN = 3 * AGES
SHORT, DDUAL, DEMAND, STOCK = range(4)
AUX = 4
IN_ROWS = MAIN + REGIONS
OUT_MAIN = 15
OUT_ROWS = OUT_MAIN + REGIONS
SPARE = STORES
HOSTS = {
    SHORT: (HOLD, HOLD + 1, HOLD + 2, HOLD + 3),
    DDUAL: (SELL, SELL + 1, SELL + 2, SELL + 3),
    DEMAND: (BAL, BAL + 1, BAL + 2, BAL + 3),
    STOCK: (HOLD + 4, HOLD + 5, SELL + 4, SELL + 5),
}
DUAL_HOST, MIXED_HOST = BAL + 4, BAL + 5
OUT_DUAL_HOST, OUT_ORDER_HOST = 12, 13
DEPOT_COLUMN = 112
DEPOT_PITCH = 16
GROUP = 8
VOLUME, PRICE, PENALTY, ORDER_COST, HOLDING_COST = range(5)

VMEM_BYTES = 20 * 1024 * 1024
f32 = jnp.float32
VM = pl.BlockSpec(memory_space=pltpu.VMEM)
SM = pl.BlockSpec(memory_space=pltpu.SMEM)
HB = pl.BlockSpec(memory_space=pltpu.HBM)
EVERY = ("region", "day", "scen")


def call(body, outs, specs, out_specs, scratch=(), micros=1):
    return pl.pallas_call(
        body,
        out_shape=outs,
        in_specs=specs,
        out_specs=out_specs,
        scratch_shapes=list(scratch),
        compiler_params=pltpu.CompilerParams(vmem_limit_bytes=VMEM_BYTES),
        cost_estimate=pl.CostEstimate(
            flops=micros * 500_000_000, bytes_accessed=micros * 3_000_000, transcendentals=0
        ),
    )


def in_hbm(array):
    return pltpu.with_memory_space_constraint(array, pltpu.HBM)


def in_vmem(array):
    return pltpu.with_memory_space_constraint(array, pltpu.VMEM)


def lane_window(start, size):
    lane = lax.broadcasted_iota(jnp.int32, (ROWS, LANES), 1)
    return (lane >= start) & (lane < start + size)


def shift_lanes(x, source, target):
    return pltpu.roll(x, (target - source) % LANES, 1)


def other_day(x):
    return pltpu.roll(x, SCENARIOS, 0)


def pack_kernel(half, place_ref, *refs):
    given, out_ref, held = refs[:13], refs[13], refs[14:27]
    packed, rows, index, came, left = refs[27:]
    (
        ship_ref,
        hold_ref,
        sell_ref,
        bal_ref,
        short_ref,
        ddual_ref,
        base_ref,
        pattern_ref,
        index_ref,
        stock_ref,
        depot_dual_ref,
        ordering_ref,
        supply_ref,
    ) = held
    coming = [pltpu.make_async_copy(given[i], held[i], came.at[i]) for i in range(13)]
    for copy in coming:
        copy.start()
    scen = place_ref[1]
    place = place_ref[0] * SCENARIOS + scen
    cols = slice(half * LANES, (half + 1) * LANES)

    coming[0].wait()

    def ship_step(b, carry):
        lanes = ship_ref[pl.ds(b * (2 * LANES) + half, LANES, stride=2), :]
        packed[pl.ds(MAIN + b, PARTS, stride=IN_ROWS), :] = lanes.T
        return carry

    lax.fori_loop(0, REGIONS, ship_step, 0)
    for copy in coming[1:]:
        copy.wait()
    index[...] = jnp.zeros_like(index)
    index[0:1, 0:STORES] = index_ref[...]
    patterns = pattern_ref.shape[0]
    chosen = lax.broadcasted_iota(jnp.int32, (patterns, LANES), 0) == index[0:1, :]
    factor = lax.dot_general(
        chosen.astype(f32),
        pattern_ref[:, cols],
        (((0,), (0,)), ((), ())),
        precision=lax.Precision.HIGHEST,
        preferred_element_type=f32,
    )
    demand = factor[0:STORES] * base_ref[:, cols]
    stock = stock_ref.at[jnp.minimum(place, AGES - 2)]

    def quarter(kind, q):
        first = QUARTER * q
        if kind == DEMAND:
            return demand[first : first + QUARTER]
        if kind == STOCK:
            return stock[first : first + QUARTER, cols]
        ref = short_ref if kind == SHORT else ddual_ref
        return ref[pl.ds(2 * first + half, QUARTER, stride=2), :]

    for slot in range(MAIN):
        ref, age = (hold_ref, sell_ref, bal_ref)[slot // AGES], slot % AGES
        block = rows.at[slot]
        block[96:LANES, :] = jnp.zeros((LANES - 96, LANES), f32)
        block[0:STORES, :] = ref[pl.ds(2 * age + half, STORES, stride=2 * AGES), :]
        for kind, hosts in HOSTS.items():
            if slot in hosts:
                block[SPARE : SPARE + QUARTER, :] = quarter(kind, hosts.index(slot))
        if slot == DUAL_HOST:
            block[SPARE : SPARE + DEPOTS, :] = depot_dual_ref[:, 0, cols]
        if slot == MIXED_HOST:
            block[SPARE : SPARE + DEPOTS, :] = jnp.where(
                scen % 2 == 0, supply_ref[:, 0, cols], ordering_ref[:, cols]
            )
        packed[pl.ds(slot, PARTS, stride=IN_ROWS), :] = block[...].T
    going = pltpu.make_async_copy(packed, out_ref, left)
    going.start()
    going.wait()


def unpack_kernel(half, in_ref, *refs):
    count = 6
    given = refs[: count * half]
    outs = refs[count * half : count * (half + 1)]
    held = refs[count * (half + 1) : count * (half + 2)]
    *earlier, came, left = refs[count * (half + 2) :]
    ship_ref, hold_ref, sell_ref, bal_ref, depot_dual_ref, ordering_ref = held
    coming = [pltpu.make_async_copy(given[i], earlier[i], came.at[i]) for i in range(len(given))]
    for copy in coming:
        copy.start()
    going = [pltpu.make_async_copy(held[i], outs[i], left.at[i]) for i in range(count)]
    pace = half + 1

    def get(slot):
        return in_ref[pl.ds(slot, PARTS, stride=OUT_ROWS), :].T

    if half:
        coming[0].wait()

    def ship_step(b, carry):
        ship_ref[pl.ds(b * (LANES * pace) + half, LANES, stride=pace), :] = get(OUT_MAIN + b)
        if half:
            ship_ref[pl.ds(b * (LANES * pace), LANES, stride=pace), :] = earlier[0][
                pl.ds(b * LANES, LANES), :
            ]
        return carry

    lax.fori_loop(0, REGIONS, ship_step, 0)
    going[0].start()
    for copy in coming[1:]:
        copy.wait()
    if half:
        for i, ref in ((1, hold_ref), (2, sell_ref), (3, bal_ref)):
            ref[pl.ds(0, STORES * AGES, stride=2), :] = earlier[i][...]
        depot_dual_ref[:, 0, :LANES] = earlier[4][...]
        ordering_ref[:, :LANES] = earlier[5][...]
    for slot in range(OUT_MAIN):
        ref, age = (hold_ref, sell_ref, bal_ref)[slot // AGES], slot % AGES
        rows = get(slot)
        ref[pl.ds(pace * age + half, STORES, stride=pace * AGES), :] = rows[0:STORES]
        if slot < 12:
            at = pace * (AGES * QUARTER * (slot % 4) + 3 + slot // 4) + half
            bal_ref[pl.ds(at, QUARTER, stride=pace * AGES), :] = rows[SPARE : SPARE + QUARTER]
        depots = rows[SPARE : SPARE + DEPOTS]
        if slot == OUT_DUAL_HOST:
            if half:
                depot_dual_ref[:, 0, LANES:] = depots
            else:
                depot_dual_ref[...] = depots
        if slot == OUT_ORDER_HOST:
            if half:
                ordering_ref[:, LANES:] = depots
            else:
                ordering_ref[...] = depots
    for copy in going[1:]:
        copy.start()
    for copy in going:
        copy.wait()


def tables_kernel(
    place_ref, store_ref, depot_ref, mask_ref, table_ref, slot_ref, keep_ref, next_ref
):
    for i in range(2):
        next_ref[i] = place_ref[i]
    column = lax.broadcasted_iota(jnp.int32, (LANES, LANES), 0)

    def step(b, carry):
        for a in range(REGIONS):
            keep = mask_ref[a, pl.ds(b, 1), :] > 0
            store = jnp.where(keep, store_ref[a, pl.ds(b, 1), :], -1)
            depot = jnp.where(keep, depot_ref[a, pl.ds(b, 1), :] + DEPOT_COLUMN, -1)
            ends = (column == store) | (column == depot)
            table_ref[b, a] = jnp.where(ends, 1.0, 0.0).astype(f32).T.astype(jnp.bfloat16)
        return carry

    lax.fori_loop(0, REGIONS, step, 0)
    for a in range(REGIONS):
        slot_ref[a] = depot_ref[a] + (a % GROUP) * DEPOT_PITCH
        keep_ref[a] = mask_ref[a].astype(f32)


def iterations_kernel(
    in_ref,
    number_ref,
    table_ref,
    store_ref,
    slot_ref,
    cost_ref,
    keep_ref,
    out_ref,
    ship,
    main,
    aux,
    flow,
    dual,
    ordering,
    supply,
    packed,
    left,
):
    sublane = lax.broadcasted_iota(jnp.int32, (ROWS, LANES), 0)
    first_day = sublane < SCENARIOS
    even = sublane % 2 == 0
    zero = jnp.zeros((ROWS, LANES), f32)
    quarters = [lane_window(QUARTER * q, QUARTER) for q in range(4)]
    spares = lane_window(SPARE, QUARTER)
    depot_spares = lane_window(SPARE, DEPOTS)

    def unfold(region, carry):
        at = region * (ROWS * IN_ROWS)
        for slot in range(MAIN):
            main[region, slot] = in_ref[pl.ds(at + slot, ROWS, stride=IN_ROWS), :]
        for b in range(REGIONS):
            ship[region, b] = in_ref[pl.ds(at + MAIN + b, ROWS, stride=IN_ROWS), :]
        for kind, hosts in HOSTS.items():
            total = zero
            for q in range(4):
                part = shift_lanes(main[region, hosts[q]], SPARE, QUARTER * q)
                total = jnp.where(quarters[q], part, total)
            aux[region, kind] = total
        return carry

    lax.fori_loop(0, REGIONS, unfold, 0)
    for group in range(2):
        duals, mixed = zero, zero
        for i in range(GROUP):
            region, at = group * GROUP + i, i * DEPOT_PITCH
            window = lane_window(at, DEPOTS)
            duals = jnp.where(window, shift_lanes(main[region, DUAL_HOST], SPARE, at), duals)
            mixed = jnp.where(window, shift_lanes(main[region, MIXED_HOST], SPARE, at), mixed)
        dual[group] = duals
        supply[group] = jnp.where(even, mixed, pltpu.roll(mixed, 1, 0))
        ordering[group] = jnp.where(even, pltpu.roll(mixed, ROWS - 1, 0), mixed)

    volume, price, penalty, order_cost = (number_ref[i] for i in range(4))
    holding_cost = [number_ref[HOLDING_COST + age] for age in range(AGES)]

    def iterate(iteration, carry):
        flow[...] = jnp.zeros_like(flow)
        later = [
            dual[group] + jnp.where(first_day, other_day(dual[group]), 0.0) for group in range(2)
        ]

        def step(b, carry):
            bal = [main[b, BAL + age] for age in range(AGES)]
            ddual, short = aux[b, DDUAL], aux[b, SHORT]
            new_short = jnp.maximum(0.0, short - PRIMAL_STEP * (penalty - ddual))
            aux[b, SHORT] = new_short
            sold, before, ended = zero, None, None
            for age in range(AGES):
                hold, sell = main[b, HOLD + age], main[b, SELL + age]
                rise = holding_cost[age] - bal[age]
                if age + 1 < AGES:
                    rise = rise + jnp.where(first_day, other_day(bal[age + 1]), 0.0)
                new_hold = jnp.maximum(0.0, hold - PRIMAL_STEP * rise)
                new_sell = jnp.maximum(0.0, sell - PRIMAL_STEP * (-price - bal[age] - ddual))
                main[b, HOLD + age] = new_hold
                main[b, SELL + age] = new_sell
                hold_bar = 2.0 * new_hold - hold
                sell_bar = 2.0 * new_sell - sell
                sold = sold + sell_bar
                if age == 0:
                    ended = bal[0] - DUAL_STEP * (hold_bar + sell_bar)
                else:
                    stock = jnp.broadcast_to(aux[b, STOCK, age - 1 : age, :], (ROWS, LANES))
                    carried = jnp.where(first_day, stock, other_day(before))
                    main[b, BAL + age] = bal[age] - DUAL_STEP * (hold_bar + sell_bar - carried)
                before = hold_bar
            short_bar = 2.0 * new_short - short
            aux[b, DDUAL] = ddual + DUAL_STEP * (aux[b, DEMAND] - sold - short_bar)
            arrived = zero
            for a in range(REGIONS):
                def spread(ref):
                    return jnp.broadcast_to(ref[a, pl.ds(b, 1), :], (ROWS, LANES))

                ends = jnp.take_along_axis(
                    bal[0], spread(store_ref), axis=1, mode="promise_in_bounds"
                ) + jnp.take_along_axis(
                    later[a // GROUP], spread(slot_ref), axis=1, mode="promise_in_bounds"
                )
                old = ship[a, b]
                new = spread(keep_ref) * jnp.maximum(
                    0.0, old - PRIMAL_STEP * (spread(cost_ref) * volume + ends)
                )
                ship[a, b] = new
                bar = 2.0 * new - old
                high = bar.astype(jnp.bfloat16).astype(f32)
                parts = jnp.concatenate([high, bar - high], axis=0).astype(jnp.bfloat16)
                sums = jnp.dot(parts, table_ref[b, a], preferred_element_type=f32)
                sums = sums[:ROWS] + sums[ROWS:]
                flow[a] = flow[a] + sums
                arrived = arrived + sums
            main[b, BAL] = ended + DUAL_STEP * arrived
            return carry

        lax.fori_loop(0, REGIONS, step, 0)
        for group in range(2):
            total = dual[group]
            for shift in (4, 2, 1):
                total = total + pltpu.roll(total, shift, 0)
            old = ordering[group]
            new = jnp.maximum(0.0, old - ORDER_STEP * (order_cost - total))
            ordering[group] = new
            net = -supply[group]
            for i in range(GROUP):
                at = i * DEPOT_PITCH
                part = shift_lanes(flow[group * GROUP + i], DEPOT_COLUMN, at)
                net = net + jnp.where(lane_window(at, DEPOTS), part, 0.0)
            running = net + jnp.where(first_day, 0.0, other_day(net))
            dual[group] = jnp.maximum(
                0.0, dual[group] + DEPOT_STEP * (running - (2.0 * new - old))
            )
        return carry

    lax.fori_loop(0, ITERS, iterate, 0)

    def fold(region, carry):
        at = region * (ROWS * OUT_ROWS)
        for slot in range(OUT_MAIN):
            tile = main[region, slot]
            if slot < 12:
                hosted = main[region, BAL + 3 + slot // 4]
                hosted = shift_lanes(hosted, QUARTER * (slot % 4), SPARE)
                tile = jnp.where(spares, hosted, tile)
            packed[pl.ds(at + slot, ROWS, stride=OUT_ROWS), :] = tile
        for b in range(REGIONS):
            packed[pl.ds(at + OUT_MAIN + b, ROWS, stride=OUT_ROWS), :] = ship[region, b]
        return carry

    lax.fori_loop(0, REGIONS, fold, 0)
    for group in range(2):
        for i in range(GROUP):
            region = group * GROUP + i
            at = region * (ROWS * OUT_ROWS)
            for host, ref in ((OUT_DUAL_HOST, dual), (OUT_ORDER_HOST, ordering)):
                part = shift_lanes(ref[group], i * DEPOT_PITCH, SPARE)
                packed[pl.ds(at + host, ROWS, stride=OUT_ROWS), :] = jnp.where(
                    depot_spares, part, main[region, host]
                )
    going = pltpu.make_async_copy(packed, out_ref, left)
    going.start()
    going.wait()


def swap(rows):
    parts = rows.reshape(PARTS, -1, 1, LANES)
    return lax.all_to_all(parts, EVERY, 0, 0, tiled=True).reshape(-1, LANES)


def per_device(
    shipments_init,
    holdings_init,
    selling_init,
    shortage_init,
    ordering_init,
    balance_dual_init,
    demand_dual_init,
    depot_dual_init,
    demand_base,
    demand_pattern,
    demand_index,
    initial_stock,
    depot_supply,
    lane_cost,
    item_volume,
    holding_cost,
    unit_price,
    short_penalty,
    order_cost,
    lane_depot,
    lane_store,
    lane_mask,
):
    place = jnp.stack([lax.axis_index("day"), lax.axis_index("scen")]).astype(jnp.int32)
    given = (
        shipments_init.reshape(-1, LANES),
        holdings_init.reshape(-1, LANES),
        selling_init.reshape(-1, LANES),
        balance_dual_init.reshape(-1, LANES),
        shortage_init.reshape(-1, LANES),
        demand_dual_init.reshape(-1, LANES),
        demand_base,
        demand_pattern,
        demand_index.reshape(1, STORES),
        jnp.transpose(initial_stock, (1, 0, 2)),
        depot_dual_init.reshape(DEPOTS, 1, SKUS),
        ordering_init,
        depot_supply,
    )
    arrived = []
    for half in range(HALVES):
        packed = call(
            functools.partial(pack_kernel, half),
            pltpu.HBM((PARTS * IN_ROWS, LANES), f32),
            [SM] + [HB] * len(given),
            HB,
            scratch=[
                *(pltpu.VMEM(array.shape, array.dtype) for array in given),
                pltpu.VMEM((PARTS * IN_ROWS, LANES), f32),
                pltpu.VMEM((MAIN, LANES, LANES), f32),
                pltpu.VMEM((8, LANES), jnp.int32),
                pltpu.SemaphoreType.DMA((len(given),)),
                pltpu.SemaphoreType.DMA,
            ],
            micros=4,
        )(place, *(in_hbm(array) for array in given))
        arrived.append(swap(packed))
        if half == 0:
            slots = (REGIONS, REGIONS, LANES)
            table, slot, keep, place = call(
                tables_kernel,
                (
                    pltpu.VMEM((REGIONS, REGIONS, LANES, LANES), jnp.bfloat16),
                    pltpu.VMEM(slots, jnp.int32),
                    pltpu.VMEM(slots, f32),
                    jax.ShapeDtypeStruct((2,), jnp.int32),
                ),
                [SM, VM, VM, VM],
                (VM, VM, VM, SM),
                micros=5,
            )(place, lane_store, lane_depot, lane_mask)
    numbers = jnp.concatenate(
        [jnp.stack([item_volume, unit_price, short_penalty, order_cost]), holding_cost], axis=0
    )
    own = (lax.axis_index("region") * DAYS + lax.axis_index("day")) * SCENARIOS
    own = own + lax.axis_index("scen")
    back = []
    for half in range(HALVES):
        mine = lax.dynamic_slice(numbers, (0, half * LANES + own), (numbers.shape[0], 1))
        back.append(
            swap(
                call(
                    iterations_kernel,
                    pltpu.HBM((PARTS * OUT_ROWS, LANES), f32),
                    [VM, SM] + [VM] * 5,
                    HB,
                    scratch=[
                        pltpu.VMEM((REGIONS, REGIONS, ROWS, LANES), f32),
                        pltpu.VMEM((REGIONS, MAIN, ROWS, LANES), f32),
                        pltpu.VMEM((REGIONS, AUX, ROWS, LANES), f32),
                        pltpu.VMEM((REGIONS, ROWS, LANES), f32),
                        pltpu.VMEM((2, ROWS, LANES), f32),
                        pltpu.VMEM((2, ROWS, LANES), f32),
                        pltpu.VMEM((2, ROWS, LANES), f32),
                        pltpu.VMEM((PARTS * OUT_ROWS, LANES), f32),
                        pltpu.SemaphoreType.DMA,
                    ],
                    micros=20,
                )(
                    arrived[half],
                    mine.reshape(-1),
                    in_vmem(table),
                    lane_store,
                    in_vmem(slot),
                    lane_cost,
                    in_vmem(keep),
                )
            )
        )
    done = ()
    for half in range(HALVES):
        pace = half + 1
        flat = (STORES * pace * AGES, LANES)
        shapes = (
            (pace * REGIONS * LANES, LANES),
            flat,
            flat,
            flat,
            (DEPOTS, 1, SKUS) if half else (DEPOTS, LANES),
            (DEPOTS, pace * LANES),
        )
        count = len(shapes)
        done = call(
            functools.partial(unpack_kernel, half),
            tuple(pltpu.HBM(shape, f32) for shape in shapes),
            [VM] + [HB] * len(done),
            (HB,) * count,
            scratch=[
                *(pltpu.VMEM(shape, f32) for shape in shapes),
                *(pltpu.VMEM(array.shape, f32) for array in done),
                pltpu.SemaphoreType.DMA((count,)),
                pltpu.SemaphoreType.DMA((count,)),
            ],
            micros=4,
        )(back[half], *(in_hbm(array) for array in done))
    shipments, holdings, selling, balance, depot_dual, ordering = done
    return (
        shipments.reshape(1, 1, REGIONS, LANES, 1, SKUS),
        holdings.reshape(1, STORES, 1, AGES, SKUS),
        selling.reshape(1, STORES, 1, AGES, SKUS),
        ordering,
        balance.reshape(1, STORES, 1, AGES, SKUS),
        depot_dual.reshape(1, DEPOTS, 1, SKUS),
    )


def solution(mesh):
    placed = (
        P("scen", "region", None, None, "day", None),
        P("scen", "region", "day", None, None),
        P("scen", "region", "day", None, None),
        P("scen", "region", "day", None),
        P("region", None),
        P("scen", "region", "day", None, None),
        P("scen", "region", "day", None),
        P("scen", "region", "day", None),
        P("region", None),
        P(),
        P("scen", "region", "day"),
        P("region", None, None),
        P("region", "day", None),
        P(),
        P(),
        P(),
        P(),
        P(),
        P(),
        P(),
        P(),
        P(),
    )
    return jax.shard_map(
        per_device,
        mesh=mesh,
        in_specs=placed,
        out_specs=(
            P("scen", "region", None, None, "day", None),
            P("scen", "region", "day", None, None),
            P("scen", "region", "day", None, None),
            P("region", None),
            P("scen", "region", "day", None, None),
            P("scen", "region", "day", None),
        ),
        check_vma=False,
    )
```

```python
import functools

import jax
import jax.numpy as jnp
from jax import lax
from jax.experimental import pallas as pl
from jax.experimental.pallas import tpu as pltpu
from jax.sharding import PartitionSpec as P

ITERS = 4
PRIMAL_STEP = 0.25
ORDER_STEP = 0.05
DUAL_STEP = 0.25
DEPOT_STEP = 0.02

REGIONS = 16
DAYS = 2
SCENARIOS = 4
ROWS = DAYS * SCENARIOS
PARTS = REGIONS * ROWS
STORES = 100
QUARTER = STORES // 4
DEPOTS = 15
LANES = 128
AGES = 6
SKUS = 256
HALVES = 2
HOLD, SELL, BAL = 0, AGES, 2 * AGES
MAIN = 3 * AGES
SHORT, DDUAL, DEMAND, STOCK = range(4)
AUX = 4
IN_ROWS = MAIN + REGIONS
OUT_MAIN = 15
OUT_ROWS = OUT_MAIN + REGIONS
SPARE = STORES
HOSTS = {
    SHORT: (HOLD, HOLD + 1, HOLD + 2, HOLD + 3),
    DDUAL: (SELL, SELL + 1, SELL + 2, SELL + 3),
    DEMAND: (BAL, BAL + 1, BAL + 2, BAL + 3),
    STOCK: (HOLD + 4, HOLD + 5, SELL + 4, SELL + 5),
}
DUAL_HOST, MIXED_HOST = BAL + 4, BAL + 5
OUT_DUAL_HOST, OUT_ORDER_HOST = 12, 13
DEPOT_COLUMN = 112
DEPOT_PITCH = 16
GROUP = 8
PIECE = 4
VOLUME, PRICE, PENALTY, ORDER_COST, HOLDING_COST = range(5)

VMEM_BYTES = 20 * 1024 * 1024
f32 = jnp.float32
VM = pl.BlockSpec(memory_space=pltpu.VMEM)
SM = pl.BlockSpec(memory_space=pltpu.SMEM)
HB = pl.BlockSpec(memory_space=pltpu.HBM)
EVERY = ("region", "day", "scen")


def call(body, outs, specs, out_specs, scratch=(), micros=1):
    return pl.pallas_call(
        body,
        out_shape=outs,
        in_specs=specs,
        out_specs=out_specs,
        scratch_shapes=list(scratch),
        compiler_params=pltpu.CompilerParams(vmem_limit_bytes=VMEM_BYTES),
        cost_estimate=pl.CostEstimate(
            flops=micros * 500_000_000, bytes_accessed=micros * 3_000_000, transcendentals=0
        ),
    )


def in_hbm(array):
    return pltpu.with_memory_space_constraint(array, pltpu.HBM)


def lane_window(start, size):
    lane = lax.broadcasted_iota(jnp.int32, (ROWS, LANES), 1)
    return (lane >= start) & (lane < start + size)


def shift_lanes(x, source, target):
    return pltpu.roll(x, (target - source) % LANES, 1)


def other_day(x):
    return pltpu.roll(x, SCENARIOS, 0)


def pack_kernel(half, place_ref, *refs):
    given, out_ref, held = refs[:13], refs[13], refs[14:27]
    packed, rows, index, came, left = refs[27:]
    (
        ship_ref,
        hold_ref,
        sell_ref,
        bal_ref,
        short_ref,
        ddual_ref,
        base_ref,
        pattern_ref,
        index_ref,
        stock_ref,
        depot_dual_ref,
        ordering_ref,
        supply_ref,
    ) = held
    coming = [pltpu.make_async_copy(given[i], held[i], came.at[i]) for i in range(13)]
    for copy in (*coming[1:], coming[0]):
        copy.start()
    scen = place_ref[1]
    place = place_ref[0] * SCENARIOS + scen
    cols = slice(half * LANES, (half + 1) * LANES)

    for copy in coming[1:]:
        copy.wait()
    index[...] = jnp.zeros_like(index)
    index[0:1, 0:STORES] = index_ref[...]
    patterns = pattern_ref.shape[0]
    chosen = lax.broadcasted_iota(jnp.int32, (patterns, LANES), 0) == index[0:1, :]
    factor = lax.dot_general(
        chosen.astype(f32),
        pattern_ref[:, cols],
        (((0,), (0,)), ((), ())),
        precision=lax.Precision.HIGHEST,
        preferred_element_type=f32,
    )
    demand = factor[0:STORES] * base_ref[:, cols]
    stock = stock_ref.at[jnp.minimum(place, AGES - 2)]

    def quarter(kind, q):
        first = QUARTER * q
        if kind == DEMAND:
            return demand[first : first + QUARTER]
        if kind == STOCK:
            return stock[first : first + QUARTER, cols]
        ref = short_ref if kind == SHORT else ddual_ref
        return ref[pl.ds(2 * first + half, QUARTER, stride=2), :]

    for slot in range(MAIN):
        ref, age = (hold_ref, sell_ref, bal_ref)[slot // AGES], slot % AGES
        block = rows.at[slot]
        block[96:LANES, :] = jnp.zeros((LANES - 96, LANES), f32)
        block[0:STORES, :] = ref[pl.ds(2 * age + half, STORES, stride=2 * AGES), :]
        for kind, hosts in HOSTS.items():
            if slot in hosts:
                block[SPARE : SPARE + QUARTER, :] = quarter(kind, hosts.index(slot))
        if slot == DUAL_HOST:
            block[SPARE : SPARE + DEPOTS, :] = depot_dual_ref[:, 0, cols]
        if slot == MIXED_HOST:
            block[SPARE : SPARE + DEPOTS, :] = jnp.where(
                scen % 2 == 0, supply_ref[:, 0, cols], ordering_ref[:, cols]
            )
        packed[pl.ds(slot, PARTS, stride=IN_ROWS), :] = block[...].T
    coming[0].wait()
    for b in range(REGIONS):
        lanes = ship_ref[pl.ds(b * (2 * LANES) + half, LANES, stride=2), :]
        packed[pl.ds(MAIN + b, PARTS, stride=IN_ROWS), :] = lanes.T
    going = pltpu.make_async_copy(packed, out_ref, left)
    going.start()
    going.wait()


def unpack_kernel(half, in_ref, *refs):
    count = 6
    given = refs[: count * half]
    outs = refs[count * half : count * (half + 1)]
    held = refs[count * (half + 1) : count * (half + 2)]
    *earlier, came, left = refs[count * (half + 2) :]
    ship_ref, hold_ref, sell_ref, bal_ref, depot_dual_ref, ordering_ref = held
    coming = [pltpu.make_async_copy(given[i], earlier[i], came.at[i]) for i in range(len(given))]
    for copy in coming:
        copy.start()
    pace = half + 1
    going = [pltpu.make_async_copy(held[i], outs[i], left.at[i]) for i in range(1, count)]
    span = PIECE * LANES * pace
    pieces = [
        pltpu.make_async_copy(
            ship_ref.at[pl.ds(i * span, span)],
            outs[0].at[pl.ds(i * span, span)],
            left.at[count + i],
        )
        for i in range(REGIONS // PIECE)
    ]

    def get(slot):
        return in_ref[pl.ds(slot, PARTS, stride=OUT_ROWS), :].T

    for slot in range(OUT_MAIN):
        ref, age = (hold_ref, sell_ref, bal_ref)[slot // AGES], slot % AGES
        rows = get(slot)
        ref[pl.ds(pace * age + half, STORES, stride=pace * AGES), :] = rows[0:STORES]
        if slot < 12:
            at = pace * (AGES * QUARTER * (slot % 4) + 3 + slot // 4) + half
            bal_ref[pl.ds(at, QUARTER, stride=pace * AGES), :] = rows[SPARE : SPARE + QUARTER]
        depots = rows[SPARE : SPARE + DEPOTS]
        if slot == OUT_DUAL_HOST:
            if half:
                depot_dual_ref[:, 0, LANES:] = depots
            else:
                depot_dual_ref[...] = depots
        if slot == OUT_ORDER_HOST:
            if half:
                ordering_ref[:, LANES:] = depots
            else:
                ordering_ref[...] = depots
    for copy in coming[1:]:
        copy.wait()
    if half:
        for i, ref in ((1, hold_ref), (2, sell_ref), (3, bal_ref)):
            ref[pl.ds(0, STORES * AGES, stride=2), :] = earlier[i][...]
        depot_dual_ref[:, 0, :LANES] = earlier[4][...]
        ordering_ref[:, :LANES] = earlier[5][...]
    for copy in going:
        copy.start()
    if half:
        coming[0].wait()
    for b in range(REGIONS):
        at = b * (LANES * pace)
        ship_ref[pl.ds(at + half, LANES, stride=pace), :] = get(OUT_MAIN + b)
        if half:
            ship_ref[pl.ds(at, LANES, stride=pace), :] = earlier[0][b * LANES : (b + 1) * LANES, :]
        if b % PIECE == PIECE - 1:
            pieces[b // PIECE].start()
    for copy in (*going, *pieces):
        copy.wait()


def tables_kernel(place_ref, store_ref, depot_ref, mask_ref, out_ref, next_ref, table, left):
    for i in range(2):
        next_ref[i] = place_ref[i]
    column = lax.broadcasted_iota(jnp.int32, (LANES, LANES), 0)

    def step(b, carry):
        for a in range(REGIONS):
            keep = mask_ref[a, pl.ds(b, 1), :] > 0
            store = jnp.where(keep, store_ref[a, pl.ds(b, 1), :], -1)
            depot = jnp.where(keep, depot_ref[a, pl.ds(b, 1), :] + DEPOT_COLUMN, -1)
            ends = (column == store) | (column == depot)
            table[b // 2, b % 2, a] = jnp.where(ends, 1.0, 0.0).astype(f32).T.astype(jnp.bfloat16)
        return carry

    lax.fori_loop(0, REGIONS, step, 0)
    going = pltpu.make_async_copy(table, out_ref, left)
    going.start()
    going.wait()


def iterations_kernel(in_ref, number_ref, table_in, *refs):
    lanes_in, out_ref, table, lanes = refs[:4], refs[4], refs[5], refs[6:10]
    slots, keeps, ship, main, aux, flow, dual, ordering, supply, packed, came, left = refs[10:]
    store_ref, depot_ref, mask_ref, cost_ref = lanes
    tables = [
        pltpu.make_async_copy(table_in.at[i], table.at[i], came.at[i]) for i in range(REGIONS // 2)
    ]
    coming = [
        pltpu.make_async_copy(lanes_in[i], lanes[i], came.at[REGIONS // 2 + i]) for i in range(4)
    ]
    for copy in (*coming, *tables):
        copy.start()
    sublane = lax.broadcasted_iota(jnp.int32, (ROWS, LANES), 0)
    first_day = sublane < SCENARIOS
    even = sublane % 2 == 0
    zero = jnp.zeros((ROWS, LANES), f32)
    quarters = [lane_window(QUARTER * q, QUARTER) for q in range(4)]
    spares = lane_window(SPARE, QUARTER)
    depot_spares = lane_window(SPARE, DEPOTS)

    def unfold(region, carry):
        at = region * (ROWS * IN_ROWS)
        for slot in range(MAIN):
            main[region, slot] = in_ref[pl.ds(at + slot, ROWS, stride=IN_ROWS), :]
        for b in range(REGIONS):
            ship[region, b] = in_ref[pl.ds(at + MAIN + b, ROWS, stride=IN_ROWS), :]
        for kind, hosts in HOSTS.items():
            total = zero
            for q in range(4):
                part = shift_lanes(main[region, hosts[q]], SPARE, QUARTER * q)
                total = jnp.where(quarters[q], part, total)
            aux[region, kind] = total
        return carry

    lax.fori_loop(0, REGIONS, unfold, 0)
    for group in range(2):
        duals, mixed = zero, zero
        for i in range(GROUP):
            region, at = group * GROUP + i, i * DEPOT_PITCH
            window = lane_window(at, DEPOTS)
            duals = jnp.where(window, shift_lanes(main[region, DUAL_HOST], SPARE, at), duals)
            mixed = jnp.where(window, shift_lanes(main[region, MIXED_HOST], SPARE, at), mixed)
        dual[group] = duals
        supply[group] = jnp.where(even, mixed, pltpu.roll(mixed, 1, 0))
        ordering[group] = jnp.where(even, pltpu.roll(mixed, ROWS - 1, 0), mixed)

    for copy in coming:
        copy.wait()
    for a in range(REGIONS):
        slots[a] = depot_ref[a] + (a % GROUP) * DEPOT_PITCH
        keeps[a] = mask_ref[a].astype(f32)
    volume, price, penalty, order_cost = (number_ref[i] for i in range(4))
    holding_cost = [number_ref[HOLDING_COST + age] for age in range(AGES)]

    def iterate(iteration, carry):
        flow[...] = jnp.zeros_like(flow)
        later = [
            dual[group] + jnp.where(first_day, other_day(dual[group]), 0.0) for group in range(2)
        ]

        def store_step(b):
            bal = [main[b, BAL + age] for age in range(AGES)]
            ddual, short = aux[b, DDUAL], aux[b, SHORT]
            new_short = jnp.maximum(0.0, short - PRIMAL_STEP * (penalty - ddual))
            aux[b, SHORT] = new_short
            sold, before, ended = zero, None, None
            for age in range(AGES):
                hold, sell = main[b, HOLD + age], main[b, SELL + age]
                rise = holding_cost[age] - bal[age]
                if age + 1 < AGES:
                    rise = rise + jnp.where(first_day, other_day(bal[age + 1]), 0.0)
                new_hold = jnp.maximum(0.0, hold - PRIMAL_STEP * rise)
                new_sell = jnp.maximum(0.0, sell - PRIMAL_STEP * (-price - bal[age] - ddual))
                main[b, HOLD + age] = new_hold
                main[b, SELL + age] = new_sell
                hold_bar = 2.0 * new_hold - hold
                sell_bar = 2.0 * new_sell - sell
                sold = sold + sell_bar
                if age == 0:
                    ended = bal[0] - DUAL_STEP * (hold_bar + sell_bar)
                else:
                    stock = jnp.broadcast_to(aux[b, STOCK, age - 1 : age, :], (ROWS, LANES))
                    carried = jnp.where(first_day, stock, other_day(before))
                    main[b, BAL + age] = bal[age] - DUAL_STEP * (hold_bar + sell_bar - carried)
                before = hold_bar
            short_bar = 2.0 * new_short - short
            aux[b, DDUAL] = ddual + DUAL_STEP * (aux[b, DEMAND] - sold - short_bar)
            return bal[0], ended

        def step(pair, carry):
            @pl.when(iteration == 0)
            def _():
                pltpu.make_async_copy(table_in.at[pair], table.at[pair], came.at[pair]).wait()

            stores = [store_step(2 * pair + i) for i in range(2)]
            arrived = [zero, zero]
            for a in range(REGIONS):
                total = None
                for i in range(2):
                    b = 2 * pair + i

                    def spread(ref):
                        return jnp.broadcast_to(ref[a, pl.ds(b, 1), :], (ROWS, LANES))

                    ends = jnp.take_along_axis(
                        stores[i][0], spread(store_ref), axis=1, mode="promise_in_bounds"
                    ) + jnp.take_along_axis(
                        later[a // GROUP], spread(slots), axis=1, mode="promise_in_bounds"
                    )
                    old = ship[a, b]
                    new = spread(keeps) * jnp.maximum(
                        0.0, old - PRIMAL_STEP * (spread(cost_ref) * volume + ends)
                    )
                    ship[a, b] = new
                    bar = 2.0 * new - old
                    high = bar.astype(jnp.bfloat16).astype(f32)
                    parts = jnp.concatenate([high, bar - high], axis=0).astype(jnp.bfloat16)
                    sums = jnp.dot(parts, table[pair, i, a], preferred_element_type=f32)
                    sums = sums[:ROWS] + sums[ROWS:]
                    arrived[i] = arrived[i] + sums
                    total = sums if i == 0 else total + sums
                flow[a] = flow[a] + total
            for i in range(2):
                main[2 * pair + i, BAL] = stores[i][1] + DUAL_STEP * arrived[i]
            return carry

        lax.fori_loop(0, REGIONS // 2, step, 0)
        for group in range(2):
            total = dual[group]
            for shift in (4, 2, 1):
                total = total + pltpu.roll(total, shift, 0)
            old = ordering[group]
            new = jnp.maximum(0.0, old - ORDER_STEP * (order_cost - total))
            ordering[group] = new
            net = -supply[group]
            for i in range(GROUP):
                at = i * DEPOT_PITCH
                part = shift_lanes(flow[group * GROUP + i], DEPOT_COLUMN, at)
                net = net + jnp.where(lane_window(at, DEPOTS), part, 0.0)
            running = net + jnp.where(first_day, 0.0, other_day(net))
            dual[group] = jnp.maximum(
                0.0, dual[group] + DEPOT_STEP * (running - (2.0 * new - old))
            )
        return carry

    lax.fori_loop(0, ITERS, iterate, 0)

    def fold(region, carry):
        at = region * (ROWS * OUT_ROWS)
        for slot in range(OUT_MAIN):
            tile = main[region, slot]
            if slot < 12:
                hosted = main[region, BAL + 3 + slot // 4]
                hosted = shift_lanes(hosted, QUARTER * (slot % 4), SPARE)
                tile = jnp.where(spares, hosted, tile)
            packed[pl.ds(at + slot, ROWS, stride=OUT_ROWS), :] = tile
        for b in range(REGIONS):
            packed[pl.ds(at + OUT_MAIN + b, ROWS, stride=OUT_ROWS), :] = ship[region, b]
        return carry

    lax.fori_loop(0, REGIONS, fold, 0)
    for group in range(2):
        for i in range(GROUP):
            region = group * GROUP + i
            at = region * (ROWS * OUT_ROWS)
            for host, ref in ((OUT_DUAL_HOST, dual), (OUT_ORDER_HOST, ordering)):
                part = shift_lanes(ref[group], i * DEPOT_PITCH, SPARE)
                packed[pl.ds(at + host, ROWS, stride=OUT_ROWS), :] = jnp.where(
                    depot_spares, part, main[region, host]
                )
    going = pltpu.make_async_copy(packed, out_ref, left)
    going.start()
    going.wait()


def swap(rows):
    parts = rows.reshape(PARTS, -1, 1, LANES)
    return lax.all_to_all(parts, EVERY, 0, 0, tiled=True).reshape(-1, LANES)


def per_device(
    shipments_init,
    holdings_init,
    selling_init,
    shortage_init,
    ordering_init,
    balance_dual_init,
    demand_dual_init,
    depot_dual_init,
    demand_base,
    demand_pattern,
    demand_index,
    initial_stock,
    depot_supply,
    lane_cost,
    item_volume,
    holding_cost,
    unit_price,
    short_penalty,
    order_cost,
    lane_depot,
    lane_store,
    lane_mask,
):
    place = jnp.stack([lax.axis_index("day"), lax.axis_index("scen")]).astype(jnp.int32)
    given = (
        shipments_init.reshape(-1, LANES),
        holdings_init.reshape(-1, LANES),
        selling_init.reshape(-1, LANES),
        balance_dual_init.reshape(-1, LANES),
        shortage_init.reshape(-1, LANES),
        demand_dual_init.reshape(-1, LANES),
        demand_base,
        demand_pattern,
        demand_index.reshape(1, STORES),
        jnp.transpose(initial_stock, (1, 0, 2)),
        depot_dual_init.reshape(DEPOTS, 1, SKUS),
        ordering_init,
        depot_supply,
    )
    table_shape = (REGIONS // 2, 2, REGIONS, LANES, LANES)
    tiles = (REGIONS, REGIONS, LANES)
    arrived = []
    for half in range(HALVES):
        packed = call(
            functools.partial(pack_kernel, half),
            pltpu.HBM((PARTS * IN_ROWS, LANES), f32),
            [SM] + [HB] * len(given),
            HB,
            scratch=[
                *(pltpu.VMEM(array.shape, array.dtype) for array in given),
                pltpu.VMEM((PARTS * IN_ROWS, LANES), f32),
                pltpu.VMEM((MAIN, LANES, LANES), f32),
                pltpu.VMEM((8, LANES), jnp.int32),
                pltpu.SemaphoreType.DMA((len(given),)),
                pltpu.SemaphoreType.DMA,
            ],
            micros=4,
        )(place, *(in_hbm(array) for array in given))
        arrived.append(swap(packed))
        if half == 0:
            table, place = call(
                tables_kernel,
                (pltpu.HBM(table_shape, jnp.bfloat16), jax.ShapeDtypeStruct((2,), jnp.int32)),
                [SM, VM, VM, VM],
                (HB, SM),
                scratch=[pltpu.VMEM(table_shape, jnp.bfloat16), pltpu.SemaphoreType.DMA],
                micros=5,
            )(place, lane_store, lane_depot, lane_mask)
    numbers = jnp.concatenate(
        [jnp.stack([item_volume, unit_price, short_penalty, order_cost]), holding_cost], axis=0
    )
    own = (lax.axis_index("region") * DAYS + lax.axis_index("day")) * SCENARIOS
    own = own + lax.axis_index("scen")
    back = []
    for half in range(HALVES):
        mine = lax.dynamic_slice(numbers, (0, half * LANES + own), (numbers.shape[0], 1))
        back.append(
            swap(
                call(
                    iterations_kernel,
                    pltpu.HBM((PARTS * OUT_ROWS, LANES), f32),
                    [VM, SM] + [HB] * 5,
                    HB,
                    scratch=[
                        pltpu.VMEM(table_shape, jnp.bfloat16),
                        *[pltpu.VMEM(tiles, jnp.int32)] * 3,
                        pltpu.VMEM(tiles, f32),
                        pltpu.VMEM(tiles, jnp.int32),
                        pltpu.VMEM(tiles, f32),
                        pltpu.VMEM((REGIONS, REGIONS, ROWS, LANES), f32),
                        pltpu.VMEM((REGIONS, MAIN, ROWS, LANES), f32),
                        pltpu.VMEM((REGIONS, AUX, ROWS, LANES), f32),
                        pltpu.VMEM((REGIONS, ROWS, LANES), f32),
                        pltpu.VMEM((2, ROWS, LANES), f32),
                        pltpu.VMEM((2, ROWS, LANES), f32),
                        pltpu.VMEM((2, ROWS, LANES), f32),
                        pltpu.VMEM((PARTS * OUT_ROWS, LANES), f32),
                        pltpu.SemaphoreType.DMA((REGIONS // 2 + 4,)),
                        pltpu.SemaphoreType.DMA,
                    ],
                    micros=20,
                )(
                    arrived[half],
                    mine.reshape(-1),
                    *(
                        in_hbm(array)
                        for array in (table, lane_store, lane_depot, lane_mask, lane_cost)
                    ),
                )
            )
        )
    done = ()
    for half in range(HALVES):
        pace = half + 1
        flat = (STORES * pace * AGES, LANES)
        shapes = (
            (pace * REGIONS * LANES, LANES),
            flat,
            flat,
            flat,
            (DEPOTS, 1, SKUS) if half else (DEPOTS, LANES),
            (DEPOTS, pace * LANES),
        )
        count = len(shapes)
        done = call(
            functools.partial(unpack_kernel, half),
            tuple(pltpu.HBM(shape, f32) for shape in shapes),
            [VM] + [HB] * len(done),
            (HB,) * count,
            scratch=[
                *(pltpu.VMEM(shape, f32) for shape in shapes),
                *(pltpu.VMEM(array.shape, f32) for array in done),
                pltpu.SemaphoreType.DMA((count,)),
                pltpu.SemaphoreType.DMA((count + REGIONS // PIECE,)),
            ],
            micros=4,
        )(back[half], *(in_hbm(array) for array in done))
    shipments, holdings, selling, balance, depot_dual, ordering = done
    return (
        shipments.reshape(1, 1, REGIONS, LANES, 1, SKUS),
        holdings.reshape(1, STORES, 1, AGES, SKUS),
        selling.reshape(1, STORES, 1, AGES, SKUS),
        ordering,
        balance.reshape(1, STORES, 1, AGES, SKUS),
        depot_dual.reshape(1, DEPOTS, 1, SKUS),
    )


def solution(mesh):
    placed = (
        P("scen", "region", None, None, "day", None),
        P("scen", "region", "day", None, None),
        P("scen", "region", "day", None, None),
        P("scen", "region", "day", None),
        P("region", None),
        P("scen", "region", "day", None, None),
        P("scen", "region", "day", None),
        P("scen", "region", "day", None),
        P("region", None),
        P(),
        P("scen", "region", "day"),
        P("region", None, None),
        P("region", "day", None),
        P(),
        P(),
        P(),
        P(),
        P(),
        P(),
        P(),
        P(),
        P(),
    )
    return jax.shard_map(
        per_device,
        mesh=mesh,
        in_specs=placed,
        out_specs=(
            P("scen", "region", None, None, "day", None),
            P("scen", "region", "day", None, None),
            P("scen", "region", "day", None, None),
            P("region", None),
            P("scen", "region", "day", None, None),
            P("scen", "region", "day", None),
        ),
        check_vma=False,
    )
```

```python
import functools

import jax
import jax.numpy as jnp
from jax import lax
from jax.experimental import pallas as pl
from jax.experimental.pallas import tpu as pltpu
from jax.sharding import PartitionSpec as P

ITERS = 4
PRIMAL_STEP = 0.25
ORDER_STEP = 0.05
DUAL_STEP = 0.25
DEPOT_STEP = 0.02

REGIONS = 16
DAYS = 2
SCENARIOS = 4
ROWS = DAYS * SCENARIOS
PARTS = REGIONS * ROWS
STORES = 100
QUARTER = STORES // 4
DEPOTS = 15
LANES = 128
AGES = 6
SKUS = 256
HALVES = 2
HOLD, SELL, BAL = 0, AGES, 2 * AGES
MAIN = 3 * AGES
SHORT, DDUAL, DEMAND, STOCK = range(4)
AUX = 4
IN_ROWS = MAIN + REGIONS
OUT_MAIN = 2 * ITERS - 1
OUT_ROWS = OUT_MAIN + REGIONS
SPARE = STORES
HOSTS = {
    SHORT: (HOLD, HOLD + 1, HOLD + 2, HOLD + 3),
    DDUAL: (SELL, SELL + 1, SELL + 2, SELL + 3),
    DEMAND: (BAL, BAL + 1, BAL + 2, BAL + 3),
    STOCK: (HOLD + 4, HOLD + 5, SELL + 4, SELL + 5),
}
DUAL_HOST, MIXED_HOST = BAL + 4, BAL + 5
OUT_DUAL_HOST, OUT_ORDER_HOST = ITERS, ITERS + 1
OWN_SHORT, OWN_DDUAL, OWN_DEMAND = MAIN, MAIN + 1, MAIN + 2
OWN = MAIN + 3
DEPOT_COLUMN = 112
DEPOT_PITCH = 16
GROUP = 8
PIECE = 4
VOLUME, PRICE, PENALTY, ORDER_COST, HOLDING_COST = range(5)

VMEM_BYTES = 20 * 1024 * 1024
f32 = jnp.float32
VM = pl.BlockSpec(memory_space=pltpu.VMEM)
SM = pl.BlockSpec(memory_space=pltpu.SMEM)
HB = pl.BlockSpec(memory_space=pltpu.HBM)
EVERY = ("region", "day", "scen")


def call(body, outs, specs, out_specs, scratch=(), micros=1):
    return pl.pallas_call(
        body,
        out_shape=outs,
        in_specs=specs,
        out_specs=out_specs,
        scratch_shapes=list(scratch),
        compiler_params=pltpu.CompilerParams(vmem_limit_bytes=VMEM_BYTES),
        cost_estimate=pl.CostEstimate(
            flops=micros * 500_000_000, bytes_accessed=micros * 3_000_000, transcendentals=0
        ),
    )


def in_hbm(array):
    return pltpu.with_memory_space_constraint(array, pltpu.HBM)


def lane_window(start, size):
    lane = lax.broadcasted_iota(jnp.int32, (ROWS, LANES), 1)
    return (lane >= start) & (lane < start + size)


def shift_lanes(x, source, target):
    return pltpu.roll(x, (target - source) % LANES, 1)


def other_day(x):
    return pltpu.roll(x, SCENARIOS, 0)


def pack_kernel(half, place_ref, *refs):
    given, out_ref, own_ref, held = refs[:13], refs[13], refs[14], refs[15:28]
    packed, own, rows, index, came, left = refs[28:]
    (
        ship_ref,
        hold_ref,
        sell_ref,
        bal_ref,
        short_ref,
        ddual_ref,
        base_ref,
        pattern_ref,
        index_ref,
        stock_ref,
        depot_dual_ref,
        ordering_ref,
        supply_ref,
    ) = held
    coming = [pltpu.make_async_copy(given[i], held[i], came.at[i]) for i in range(13)]
    for copy in (*coming[1:], coming[0]):
        copy.start()
    scen = place_ref[1]
    place = place_ref[0] * SCENARIOS + scen
    cols = slice(half * LANES, (half + 1) * LANES)

    for copy in coming[1:]:
        copy.wait()
    index[...] = jnp.zeros_like(index)
    index[0:1, 0:STORES] = index_ref[...]
    patterns = pattern_ref.shape[0]
    chosen = lax.broadcasted_iota(jnp.int32, (patterns, LANES), 0) == index[0:1, :]
    factor = lax.dot_general(
        chosen.astype(f32),
        pattern_ref[:, cols],
        (((0,), (0,)), ((), ())),
        precision=lax.Precision.HIGHEST,
        preferred_element_type=f32,
    )
    demand = factor[0:STORES] * base_ref[:, cols]
    stock = stock_ref.at[jnp.minimum(place, AGES - 2)]

    def quarter(kind, q):
        first = QUARTER * q
        if kind == DEMAND:
            return demand[first : first + QUARTER]
        if kind == STOCK:
            return stock[first : first + QUARTER, cols]
        ref = short_ref if kind == SHORT else ddual_ref
        return ref[pl.ds(2 * first + half, QUARTER, stride=2), :]

    for slot in range(MAIN):
        ref, age = (hold_ref, sell_ref, bal_ref)[slot // AGES], slot % AGES
        block = rows.at[slot]
        block[96:LANES, :] = jnp.zeros((LANES - 96, LANES), f32)
        values = ref[pl.ds(2 * age + half, STORES, stride=2 * AGES), :]
        block[0:STORES, :] = values
        own[slot * STORES : (slot + 1) * STORES, :] = values
        for kind, hosts in HOSTS.items():
            if slot in hosts:
                block[SPARE : SPARE + QUARTER, :] = quarter(kind, hosts.index(slot))
        if slot == DUAL_HOST:
            block[SPARE : SPARE + DEPOTS, :] = depot_dual_ref[:, 0, cols]
        if slot == MIXED_HOST:
            block[SPARE : SPARE + DEPOTS, :] = jnp.where(
                scen % 2 == 0, supply_ref[:, 0, cols], ordering_ref[:, cols]
            )
        packed[pl.ds(slot, PARTS, stride=IN_ROWS), :] = block[...].T
    for slot, values in (
        (OWN_SHORT, short_ref[pl.ds(half, STORES, stride=2), :]),
        (OWN_DDUAL, ddual_ref[pl.ds(half, STORES, stride=2), :]),
        (OWN_DEMAND, demand),
    ):
        own[slot * STORES : (slot + 1) * STORES, :] = values
    kept = pltpu.make_async_copy(own, own_ref, left.at[1])
    kept.start()
    coming[0].wait()
    for b in range(REGIONS):
        lanes = ship_ref[pl.ds(b * (2 * LANES) + half, LANES, stride=2), :]
        packed[pl.ds(MAIN + b, PARTS, stride=IN_ROWS), :] = lanes.T
    going = pltpu.make_async_copy(packed, out_ref, left.at[0])
    going.start()
    kept.wait()
    going.wait()


def unpack_kernel(half, place_ref, in_ref, *refs):
    count = 6
    local, refs = refs[:3], refs[3:]
    given = refs[: count * half]
    outs = refs[count * half : count * (half + 1)]
    held = refs[count * (half + 1) : count * (half + 2)]
    *earlier, both_ref, stock_ref, number_ref, stocks, arrivals, came, left = refs[
        count * (half + 2) :
    ]
    cols = slice(half * LANES, (half + 1) * LANES)
    ship_ref, hold_ref, sell_ref, bal_ref, depot_dual_ref, ordering_ref = held
    coming = [pltpu.make_async_copy(given[i], earlier[i], came.at[i]) for i in range(len(given))]
    locals_in = [
        pltpu.make_async_copy(local[i], ref, came.at[count + i])
        for i, ref in enumerate((both_ref, stock_ref, number_ref))
    ]
    for copy in (*coming, *locals_in):
        copy.start()
    pace = half + 1
    going = [pltpu.make_async_copy(held[i], outs[i], left.at[i]) for i in range(1, count)]
    span = PIECE * LANES * pace
    pieces = [
        pltpu.make_async_copy(
            ship_ref.at[pl.ds(i * span, span)],
            outs[0].at[pl.ds(i * span, span)],
            left.at[count + i],
        )
        for i in range(REGIONS // PIECE)
    ]

    def get(slot):
        return in_ref[pl.ds(slot, PARTS, stride=OUT_ROWS), :].T

    if half:
        coming[0].wait()
    for b in range(REGIONS):
        at = b * (LANES * pace)
        ship_ref[pl.ds(at + half, LANES, stride=pace), :] = get(OUT_MAIN + b)
        if half:
            ship_ref[pl.ds(at, LANES, stride=pace), :] = earlier[0][b * LANES : (b + 1) * LANES, :]
        if b % PIECE == PIECE - 1:
            pieces[b // PIECE].start()
    for copy in (*coming[1:], *locals_in):
        copy.wait()
    if half:
        for i, ref in ((1, hold_ref), (2, sell_ref), (3, bal_ref)):
            ref[pl.ds(0, STORES * AGES, stride=2), :] = earlier[i][...]
        depot_dual_ref[:, 0, :LANES] = earlier[4][...]
        ordering_ref[:, :LANES] = earlier[5][...]
    for slot in range(OUT_MAIN):
        arrivals[slot] = get(slot)
        if slot < 4:
            arrivals[OUT_MAIN, QUARTER * slot : QUARTER * (slot + 1), :] = arrivals[
                slot, SPARE : SPARE + QUARTER, :
            ]
        depots = arrivals[slot, SPARE : SPARE + DEPOTS, :]
        if slot == OUT_DUAL_HOST:
            if half:
                depot_dual_ref[:, 0, LANES:] = depots
            else:
                depot_dual_ref[...] = depots
        if slot == OUT_ORDER_HOST:
            if half:
                ordering_ref[:, LANES:] = depots
            else:
                ordering_ref[...] = depots
    for age in range(AGES - 1):
        stocks[age * STORES : (age + 1) * STORES, :] = stock_ref[age, :, cols]
    first_day = place_ref[0] == 0

    def number(row):
        return jnp.broadcast_to(number_ref[row : row + 1, cols], (ROWS, LANES))

    def by_day(mine, other):
        return jnp.where(first_day, mine, other), jnp.where(first_day, other, mine)

    def stores_step(block, carry):
        at = jnp.minimum(ROWS * block, STORES - ROWS)

        def load(slot):
            return [
                both_ref[pl.ds((day * OWN + slot) * STORES + at, ROWS), :] for day in range(DAYS)
            ]

        hold, sell, bal = (
            [list(days) for days in zip(*(load(first + age) for age in range(AGES)))]
            for first in (HOLD, SELL, BAL)
        )
        short, ddual, demand = (list(load(slot)) for slot in (OWN_SHORT, OWN_DDUAL, OWN_DEMAND))
        stock = [stocks[pl.ds(age * STORES + at, ROWS), :] for age in range(AGES - 1)]
        span = pl.ds(at, ROWS)
        price, penalty = number(PRICE), number(PENALTY)
        holding_cost = [number(HOLDING_COST + age) for age in range(AGES)]
        for iteration in range(ITERS):
            arrived = by_day(arrivals[iteration, span, :], arrivals[ITERS + iteration, span, :])
            before, new_bal = None, [None, None]
            for t in range(DAYS):
                new_short = jnp.maximum(0.0, short[t] - PRIMAL_STEP * (penalty - ddual[t]))
                sold, bars, after = None, [], []
                for age in range(AGES):
                    here = bal[t][age]
                    rise = holding_cost[age] - here
                    if t == 0 and age + 1 < AGES:
                        rise = rise + bal[1][age + 1]
                    new_hold = jnp.maximum(0.0, hold[t][age] - PRIMAL_STEP * rise)
                    new_sell = jnp.maximum(
                        0.0, sell[t][age] - PRIMAL_STEP * (-price - here - ddual[t])
                    )
                    bars.append(2.0 * new_hold - hold[t][age])
                    sell_bar = 2.0 * new_sell - sell[t][age]
                    sold = sell_bar if sold is None else sold + sell_bar
                    hold[t][age], sell[t][age] = new_hold, new_sell
                    if age == 0:
                        carried = arrived[t]
                    else:
                        carried = before[age - 1] if t else stock[age - 1]
                    after.append(here - DUAL_STEP * (bars[age] + sell_bar - carried))
                short_bar = 2.0 * new_short - short[t]
                ddual[t] = ddual[t] + DUAL_STEP * (demand[t] - sold - short_bar)
                short[t] = new_short
                before, new_bal[t] = bars, after
            bal = new_bal
        for values, ref in ((hold, hold_ref), (sell, sell_ref), (bal, bal_ref)):
            for age in range(AGES):
                rows = pl.ds(pace * (at * AGES + age) + half, ROWS, stride=pace * AGES)
                ref[rows, :] = jnp.where(first_day, values[0][age], values[1][age])
        return carry

    lax.fori_loop(0, pl.cdiv(STORES, ROWS), stores_step, 0)
    for copy in going:
        copy.start()
    for copy in (*going, *pieces):
        copy.wait()


def tables_kernel(place_ref, store_ref, depot_ref, mask_ref, out_ref, next_ref, table, left):
    for i in range(2):
        next_ref[i] = place_ref[i]
    column = lax.broadcasted_iota(jnp.int32, (LANES, LANES), 0)

    def step(b, carry):
        for a in range(REGIONS):
            keep = mask_ref[a, pl.ds(b, 1), :] > 0
            store = jnp.where(keep, store_ref[a, pl.ds(b, 1), :], -1)
            depot = jnp.where(keep, depot_ref[a, pl.ds(b, 1), :] + DEPOT_COLUMN, -1)
            ends = (column == store) | (column == depot)
            table[b // 2, b % 2, a] = jnp.where(ends, 1.0, 0.0).astype(f32).T.astype(jnp.bfloat16)
        return carry

    lax.fori_loop(0, REGIONS, step, 0)
    going = pltpu.make_async_copy(table, out_ref, left)
    going.start()
    going.wait()


def iterations_kernel(in_ref, number_ref, table_in, *refs):
    lanes_in, out_ref, table, lanes = refs[:4], refs[4], refs[5], refs[6:10]
    slots, keeps, ship, main, aux, arrivals, flow, dual, ordering, supply, packed, came, left = refs[
        10:
    ]
    store_ref, depot_ref, mask_ref, cost_ref = lanes
    tables = [
        pltpu.make_async_copy(table_in.at[i], table.at[i], came.at[i]) for i in range(REGIONS // 2)
    ]
    coming = [
        pltpu.make_async_copy(lanes_in[i], lanes[i], came.at[REGIONS // 2 + i]) for i in range(4)
    ]
    for copy in (*coming, *tables):
        copy.start()
    sublane = lax.broadcasted_iota(jnp.int32, (ROWS, LANES), 0)
    first_day = sublane < SCENARIOS
    even = sublane % 2 == 0
    zero = jnp.zeros((ROWS, LANES), f32)
    quarters = [lane_window(QUARTER * q, QUARTER) for q in range(4)]
    spares = lane_window(SPARE, QUARTER)
    depot_spares = lane_window(SPARE, DEPOTS)

    def unfold(region, carry):
        at = region * (ROWS * IN_ROWS)
        for slot in range(MAIN):
            main[region, slot] = in_ref[pl.ds(at + slot, ROWS, stride=IN_ROWS), :]
        for b in range(REGIONS):
            ship[region, b] = in_ref[pl.ds(at + MAIN + b, ROWS, stride=IN_ROWS), :]
        for kind, hosts in HOSTS.items():
            total = zero
            for q in range(4):
                part = shift_lanes(main[region, hosts[q]], SPARE, QUARTER * q)
                total = jnp.where(quarters[q], part, total)
            aux[region, kind] = total
        return carry

    lax.fori_loop(0, REGIONS, unfold, 0)
    for group in range(2):
        duals, mixed = zero, zero
        for i in range(GROUP):
            region, at = group * GROUP + i, i * DEPOT_PITCH
            window = lane_window(at, DEPOTS)
            duals = jnp.where(window, shift_lanes(main[region, DUAL_HOST], SPARE, at), duals)
            mixed = jnp.where(window, shift_lanes(main[region, MIXED_HOST], SPARE, at), mixed)
        dual[group] = duals
        supply[group] = jnp.where(even, mixed, pltpu.roll(mixed, 1, 0))
        ordering[group] = jnp.where(even, pltpu.roll(mixed, ROWS - 1, 0), mixed)

    for copy in coming:
        copy.wait()
    for a in range(REGIONS):
        slots[a] = depot_ref[a] + (a % GROUP) * DEPOT_PITCH
        keeps[a] = mask_ref[a].astype(f32)
    volume, price, penalty, order_cost = (number_ref[i] for i in range(4))
    holding_cost = [number_ref[HOLDING_COST + age] for age in range(AGES)]

    def iterate(iteration, carry):
        flow[...] = jnp.zeros_like(flow)
        later = [
            dual[group] + jnp.where(first_day, other_day(dual[group]), 0.0) for group in range(2)
        ]

        def store_step(b):
            bal = [main[b, BAL + age] for age in range(AGES)]
            ddual, short = aux[b, DDUAL], aux[b, SHORT]
            new_short = jnp.maximum(0.0, short - PRIMAL_STEP * (penalty - ddual))
            aux[b, SHORT] = new_short
            sold, before, ended = zero, None, None
            for age in range(AGES):
                hold, sell = main[b, HOLD + age], main[b, SELL + age]
                rise = holding_cost[age] - bal[age]
                if age + 1 < AGES:
                    rise = rise + jnp.where(first_day, other_day(bal[age + 1]), 0.0)
                new_hold = jnp.maximum(0.0, hold - PRIMAL_STEP * rise)
                new_sell = jnp.maximum(0.0, sell - PRIMAL_STEP * (-price - bal[age] - ddual))
                main[b, HOLD + age] = new_hold
                main[b, SELL + age] = new_sell
                hold_bar = 2.0 * new_hold - hold
                sell_bar = 2.0 * new_sell - sell
                sold = sold + sell_bar
                if age == 0:
                    ended = bal[0] - DUAL_STEP * (hold_bar + sell_bar)
                else:
                    stock = jnp.broadcast_to(aux[b, STOCK, age - 1 : age, :], (ROWS, LANES))
                    carried = jnp.where(first_day, stock, other_day(before))
                    main[b, BAL + age] = bal[age] - DUAL_STEP * (hold_bar + sell_bar - carried)
                before = hold_bar
            short_bar = 2.0 * new_short - short
            aux[b, DDUAL] = ddual + DUAL_STEP * (aux[b, DEMAND] - sold - short_bar)
            return bal[0], ended

        def step(pair, carry):
            @pl.when(iteration == 0)
            def _():
                pltpu.make_async_copy(table_in.at[pair], table.at[pair], came.at[pair]).wait()

            stores = [store_step(2 * pair + i) for i in range(2)]
            arrived = [zero, zero]
            for a in range(REGIONS):
                total = None
                for i in range(2):
                    b = 2 * pair + i

                    def spread(ref):
                        return jnp.broadcast_to(ref[a, pl.ds(b, 1), :], (ROWS, LANES))

                    ends = jnp.take_along_axis(
                        stores[i][0], spread(store_ref), axis=1, mode="promise_in_bounds"
                    ) + jnp.take_along_axis(
                        later[a // GROUP], spread(slots), axis=1, mode="promise_in_bounds"
                    )
                    old = ship[a, b]
                    new = spread(keeps) * jnp.maximum(
                        0.0, old - PRIMAL_STEP * (spread(cost_ref) * volume + ends)
                    )
                    ship[a, b] = new
                    bar = 2.0 * new - old
                    high = bar.astype(jnp.bfloat16).astype(f32)
                    parts = jnp.concatenate([high, bar - high], axis=0).astype(jnp.bfloat16)
                    sums = jnp.dot(parts, table[pair, i, a], preferred_element_type=f32)
                    sums = sums[:ROWS] + sums[ROWS:]
                    arrived[i] = arrived[i] + sums
                    total = sums if i == 0 else total + sums
                flow[a] = flow[a] + total
            for i in range(2):
                main[2 * pair + i, BAL] = stores[i][1] + DUAL_STEP * arrived[i]
                arrivals[2 * pair + i, iteration] = arrived[i]
            return carry

        lax.fori_loop(0, REGIONS // 2, step, 0)
        for group in range(2):
            total = dual[group]
            for shift in (4, 2, 1):
                total = total + pltpu.roll(total, shift, 0)
            old = ordering[group]
            new = jnp.maximum(0.0, old - ORDER_STEP * (order_cost - total))
            ordering[group] = new
            net = -supply[group]
            for i in range(GROUP):
                at = i * DEPOT_PITCH
                part = shift_lanes(flow[group * GROUP + i], DEPOT_COLUMN, at)
                net = net + jnp.where(lane_window(at, DEPOTS), part, 0.0)
            running = net + jnp.where(first_day, 0.0, other_day(net))
            dual[group] = jnp.maximum(
                0.0, dual[group] + DEPOT_STEP * (running - (2.0 * new - old))
            )
        return carry

    lax.fori_loop(0, ITERS, iterate, 0)

    def fold(region, carry):
        at = region * (ROWS * OUT_ROWS)
        rest = other_day(arrivals[region, ITERS - 1])
        for i in range(ITERS):
            hosted = shift_lanes(rest, QUARTER * i, SPARE)
            packed[pl.ds(at + i, ROWS, stride=OUT_ROWS), :] = jnp.where(
                spares, hosted, arrivals[region, i]
            )
            if i + 1 < ITERS:
                packed[pl.ds(at + ITERS + i, ROWS, stride=OUT_ROWS), :] = other_day(
                    arrivals[region, i]
                )
        for b in range(REGIONS):
            packed[pl.ds(at + OUT_MAIN + b, ROWS, stride=OUT_ROWS), :] = ship[region, b]
        return carry

    lax.fori_loop(0, REGIONS, fold, 0)
    for group in range(2):
        for i in range(GROUP):
            region = group * GROUP + i
            at = region * (ROWS * OUT_ROWS)
            for host, ref in ((OUT_DUAL_HOST, dual), (OUT_ORDER_HOST, ordering)):
                part = shift_lanes(ref[group], i * DEPOT_PITCH, SPARE)
                packed[pl.ds(at + host, ROWS, stride=OUT_ROWS), :] = jnp.where(
                    depot_spares, part, other_day(arrivals[region, host - ITERS])
                )
    going = pltpu.make_async_copy(packed, out_ref, left)
    going.start()
    going.wait()


def swap(rows):
    parts = rows.reshape(PARTS, -1, 1, LANES)
    return lax.all_to_all(parts, EVERY, 0, 0, tiled=True).reshape(-1, LANES)


def per_device(
    shipments_init,
    holdings_init,
    selling_init,
    shortage_init,
    ordering_init,
    balance_dual_init,
    demand_dual_init,
    depot_dual_init,
    demand_base,
    demand_pattern,
    demand_index,
    initial_stock,
    depot_supply,
    lane_cost,
    item_volume,
    holding_cost,
    unit_price,
    short_penalty,
    order_cost,
    lane_depot,
    lane_store,
    lane_mask,
):
    place = jnp.stack([lax.axis_index("day"), lax.axis_index("scen")]).astype(jnp.int32)
    given = (
        shipments_init.reshape(-1, LANES),
        holdings_init.reshape(-1, LANES),
        selling_init.reshape(-1, LANES),
        balance_dual_init.reshape(-1, LANES),
        shortage_init.reshape(-1, LANES),
        demand_dual_init.reshape(-1, LANES),
        demand_base,
        demand_pattern,
        demand_index.reshape(1, STORES),
        jnp.transpose(initial_stock, (1, 0, 2)),
        depot_dual_init.reshape(DEPOTS, 1, SKUS),
        ordering_init,
        depot_supply,
    )
    table_shape = (REGIONS // 2, 2, REGIONS, LANES, LANES)
    tiles = (REGIONS, REGIONS, LANES)
    start = place
    arrived, both_days = [], []
    for half in range(HALVES):
        packed, own_stores = call(
            functools.partial(pack_kernel, half),
            (pltpu.HBM((PARTS * IN_ROWS, LANES), f32), pltpu.HBM((OWN * STORES, LANES), f32)),
            [SM] + [HB] * len(given),
            (HB, HB),
            scratch=[
                *(pltpu.VMEM(array.shape, array.dtype) for array in given),
                pltpu.VMEM((PARTS * IN_ROWS, LANES), f32),
                pltpu.VMEM((OWN * STORES, LANES), f32),
                pltpu.VMEM((MAIN, LANES, LANES), f32),
                pltpu.VMEM((8, LANES), jnp.int32),
                pltpu.SemaphoreType.DMA((len(given),)),
                pltpu.SemaphoreType.DMA((2,)),
            ],
            micros=4,
        )(place, *(in_hbm(array) for array in given))
        arrived.append(swap(packed))
        both_days.append(lax.all_gather(own_stores, "day", axis=0, tiled=True))
        if half == 0:
            table, place = call(
                tables_kernel,
                (pltpu.HBM(table_shape, jnp.bfloat16), jax.ShapeDtypeStruct((2,), jnp.int32)),
                [SM, VM, VM, VM],
                (HB, SM),
                scratch=[pltpu.VMEM(table_shape, jnp.bfloat16), pltpu.SemaphoreType.DMA],
                micros=5,
            )(place, lane_store, lane_depot, lane_mask)
    numbers = jnp.concatenate(
        [jnp.stack([item_volume, unit_price, short_penalty, order_cost]), holding_cost], axis=0
    )
    own = (lax.axis_index("region") * DAYS + lax.axis_index("day")) * SCENARIOS
    own = own + lax.axis_index("scen")
    back = []
    for half in range(HALVES):
        mine = lax.dynamic_slice(numbers, (0, half * LANES + own), (numbers.shape[0], 1))
        back.append(
            swap(
                call(
                    iterations_kernel,
                    pltpu.HBM((PARTS * OUT_ROWS, LANES), f32),
                    [VM, SM] + [HB] * 5,
                    HB,
                    scratch=[
                        pltpu.VMEM(table_shape, jnp.bfloat16),
                        *[pltpu.VMEM(tiles, jnp.int32)] * 3,
                        pltpu.VMEM(tiles, f32),
                        pltpu.VMEM(tiles, jnp.int32),
                        pltpu.VMEM(tiles, f32),
                        pltpu.VMEM((REGIONS, REGIONS, ROWS, LANES), f32),
                        pltpu.VMEM((REGIONS, MAIN, ROWS, LANES), f32),
                        pltpu.VMEM((REGIONS, AUX, ROWS, LANES), f32),
                        pltpu.VMEM((REGIONS, ITERS, ROWS, LANES), f32),
                        pltpu.VMEM((REGIONS, ROWS, LANES), f32),
                        pltpu.VMEM((2, ROWS, LANES), f32),
                        pltpu.VMEM((2, ROWS, LANES), f32),
                        pltpu.VMEM((2, ROWS, LANES), f32),
                        pltpu.VMEM((PARTS * OUT_ROWS, LANES), f32),
                        pltpu.SemaphoreType.DMA((REGIONS // 2 + 4,)),
                        pltpu.SemaphoreType.DMA,
                    ],
                    micros=20,
                )(
                    arrived[half],
                    mine.reshape(-1),
                    *(
                        in_hbm(array)
                        for array in (table, lane_store, lane_depot, lane_mask, lane_cost)
                    ),
                )
            )
        )
    done = ()
    for half in range(HALVES):
        pace = half + 1
        flat = (STORES * pace * AGES, LANES)
        shapes = (
            (pace * REGIONS * LANES, LANES),
            flat,
            flat,
            flat,
            (DEPOTS, 1, SKUS) if half else (DEPOTS, LANES),
            (DEPOTS, pace * LANES),
        )
        count = len(shapes)
        done = call(
            functools.partial(unpack_kernel, half),
            tuple(pltpu.HBM(shape, f32) for shape in shapes),
            [SM, VM] + [HB] * (3 + len(done)),
            (HB,) * count,
            scratch=[
                *(pltpu.VMEM(shape, f32) for shape in shapes),
                *(pltpu.VMEM(array.shape, f32) for array in done),
                *(pltpu.VMEM(array.shape, f32) for array in (both_days[half], given[9], numbers)),
                pltpu.VMEM(((AGES - 1) * STORES, LANES), f32),
                pltpu.VMEM((2 * ITERS, LANES, LANES), f32),
                pltpu.SemaphoreType.DMA((count + 4,)),
                pltpu.SemaphoreType.DMA((count + REGIONS // PIECE,)),
            ],
            micros=8,
        )(
            start,
            back[half],
            *(in_hbm(array) for array in (both_days[half], given[9], numbers, *done)),
        )
    shipments, holdings, selling, balance, depot_dual, ordering = done
    return (
        shipments.reshape(1, 1, REGIONS, LANES, 1, SKUS),
        holdings.reshape(1, STORES, 1, AGES, SKUS),
        selling.reshape(1, STORES, 1, AGES, SKUS),
        ordering,
        balance.reshape(1, STORES, 1, AGES, SKUS),
        depot_dual.reshape(1, DEPOTS, 1, SKUS),
    )


def solution(mesh):
    placed = (
        P("scen", "region", None, None, "day", None),
        P("scen", "region", "day", None, None),
        P("scen", "region", "day", None, None),
        P("scen", "region", "day", None),
        P("region", None),
        P("scen", "region", "day", None, None),
        P("scen", "region", "day", None),
        P("scen", "region", "day", None),
        P("region", None),
        P(),
        P("scen", "region", "day"),
        P("region", None, None),
        P("region", "day", None),
        P(),
        P(),
        P(),
        P(),
        P(),
        P(),
        P(),
        P(),
        P(),
    )
    return jax.shard_map(
        per_device,
        mesh=mesh,
        in_specs=placed,
        out_specs=(
            P("scen", "region", None, None, "day", None),
            P("scen", "region", "day", None, None),
            P("scen", "region", "day", None, None),
            P("region", None),
            P("scen", "region", "day", None, None),
            P("scen", "region", "day", None),
        ),
        check_vma=False,
    )
```

```python
import functools

import jax
import jax.numpy as jnp
from jax import lax
from jax.experimental import pallas as pl
from jax.experimental.pallas import tpu as pltpu
from jax.sharding import PartitionSpec as P

ITERS = 4
PRIMAL_STEP = 0.25
ORDER_STEP = 0.05
DUAL_STEP = 0.25
DEPOT_STEP = 0.02

REGIONS = 16
DAYS = 2
SCENARIOS = 4
ROWS = DAYS * SCENARIOS
PARTS = REGIONS * ROWS
STORES = 100
QUARTER = STORES // 4
DEPOTS = 15
LANES = 128
AGES = 6
SKUS = 256
HALVES = 2
HOLD, SELL, BAL = 0, AGES, 2 * AGES
MAIN = 3 * AGES
SHORT, DDUAL, DEMAND, STOCK = range(4)
AUX = 4
IN_ROWS = MAIN + REGIONS
OUT_MAIN = 15
OUT_ROWS = OUT_MAIN + REGIONS
SPARE = STORES
HOSTS = {
    SHORT: (HOLD, HOLD + 1, HOLD + 2, HOLD + 3),
    DDUAL: (SELL, SELL + 1, SELL + 2, SELL + 3),
    DEMAND: (BAL, BAL + 1, BAL + 2, BAL + 3),
    STOCK: (HOLD + 4, HOLD + 5, SELL + 4, SELL + 5),
}
DUAL_HOST, MIXED_HOST = BAL + 4, BAL + 5
OUT_DUAL_HOST, OUT_ORDER_HOST = 12, 13
DEPOT_COLUMN = 112
DEPOT_PITCH = 16
GROUP = 8
PIECE = 4
VOLUME, PRICE, PENALTY, ORDER_COST, HOLDING_COST = range(5)

VMEM_BYTES = 20 * 1024 * 1024
f32 = jnp.float32
VM = pl.BlockSpec(memory_space=pltpu.VMEM)
SM = pl.BlockSpec(memory_space=pltpu.SMEM)
HB = pl.BlockSpec(memory_space=pltpu.HBM)
EVERY = ("region", "day", "scen")


def call(body, outs, specs, out_specs, scratch=(), micros=1):
    return pl.pallas_call(
        body,
        out_shape=outs,
        in_specs=specs,
        out_specs=out_specs,
        scratch_shapes=list(scratch),
        compiler_params=pltpu.CompilerParams(vmem_limit_bytes=VMEM_BYTES),
        cost_estimate=pl.CostEstimate(
            flops=micros * 500_000_000, bytes_accessed=micros * 3_000_000, transcendentals=0
        ),
    )


def in_hbm(array):
    return pltpu.with_memory_space_constraint(array, pltpu.HBM)


def in_vmem(array):
    return pltpu.with_memory_space_constraint(array, pltpu.VMEM)


def lane_window(start, size):
    lane = lax.broadcasted_iota(jnp.int32, (ROWS, LANES), 1)
    return (lane >= start) & (lane < start + size)


def shift_lanes(x, source, target):
    return pltpu.roll(x, (target - source) % LANES, 1)


def other_day(x):
    return pltpu.roll(x, SCENARIOS, 0)


def pack_kernel(half, place_ref, *refs):
    given, out_ref, held = refs[:13], refs[13], refs[14:27]
    packed, rows, index, came, left = refs[27:]
    (
        ship_ref,
        hold_ref,
        sell_ref,
        bal_ref,
        short_ref,
        ddual_ref,
        base_ref,
        pattern_ref,
        index_ref,
        stock_ref,
        depot_dual_ref,
        ordering_ref,
        supply_ref,
    ) = held
    coming = [pltpu.make_async_copy(given[i], held[i], came.at[i]) for i in range(13)]
    for copy in (*coming[1:], coming[0]):
        copy.start()
    scen = place_ref[1]
    place = place_ref[0] * SCENARIOS + scen
    cols = slice(half * LANES, (half + 1) * LANES)

    for copy in coming[1:]:
        copy.wait()
    index[...] = jnp.zeros_like(index)
    index[0:1, 0:STORES] = index_ref[...]
    patterns = pattern_ref.shape[0]
    chosen = lax.broadcasted_iota(jnp.int32, (patterns, LANES), 0) == index[0:1, :]
    factor = lax.dot_general(
        chosen.astype(f32),
        pattern_ref[:, cols],
        (((0,), (0,)), ((), ())),
        precision=lax.Precision.HIGHEST,
        preferred_element_type=f32,
    )
    demand = factor[0:STORES] * base_ref[:, cols]
    stock = stock_ref.at[jnp.minimum(place, AGES - 2)]

    def quarter(kind, q):
        first = QUARTER * q
        if kind == DEMAND:
            return demand[first : first + QUARTER]
        if kind == STOCK:
            return stock[first : first + QUARTER, cols]
        ref = short_ref if kind == SHORT else ddual_ref
        return ref[pl.ds(2 * first + half, QUARTER, stride=2), :]

    for slot in range(MAIN):
        ref, age = (hold_ref, sell_ref, bal_ref)[slot // AGES], slot % AGES
        block = rows.at[slot]
        block[96:LANES, :] = jnp.zeros((LANES - 96, LANES), f32)
        block[0:STORES, :] = ref[pl.ds(2 * age + half, STORES, stride=2 * AGES), :]
        for kind, hosts in HOSTS.items():
            if slot in hosts:
                block[SPARE : SPARE + QUARTER, :] = quarter(kind, hosts.index(slot))
        if slot == DUAL_HOST:
            block[SPARE : SPARE + DEPOTS, :] = depot_dual_ref[:, 0, cols]
        if slot == MIXED_HOST:
            block[SPARE : SPARE + DEPOTS, :] = jnp.where(
                scen % 2 == 0, supply_ref[:, 0, cols], ordering_ref[:, cols]
            )
        packed[pl.ds(slot, PARTS, stride=IN_ROWS), :] = block[...].T
    coming[0].wait()
    for b in range(REGIONS):
        lanes = ship_ref[pl.ds(b * (2 * LANES) + half, LANES, stride=2), :]
        packed[pl.ds(MAIN + b, PARTS, stride=IN_ROWS), :] = lanes.T
    going = pltpu.make_async_copy(packed, out_ref, left)
    going.start()
    going.wait()


def unpack_kernel(half, in_ref, *refs):
    count = 6
    given = refs[: count * half]
    outs = refs[count * half : count * (half + 1)]
    held = refs[count * (half + 1) : count * (half + 2)]
    *earlier, came, left = refs[count * (half + 2) :]
    ship_ref, hold_ref, sell_ref, bal_ref, depot_dual_ref, ordering_ref = held
    coming = [pltpu.make_async_copy(given[i], earlier[i], came.at[i]) for i in range(len(given))]
    for copy in coming:
        copy.start()
    pace = half + 1
    going = [pltpu.make_async_copy(held[i], outs[i], left.at[i]) for i in range(1, count)]
    span = PIECE * LANES * pace
    pieces = [
        pltpu.make_async_copy(
            ship_ref.at[pl.ds(i * span, span)],
            outs[0].at[pl.ds(i * span, span)],
            left.at[count + i],
        )
        for i in range(REGIONS // PIECE)
    ]

    def get(slot):
        return in_ref[pl.ds(slot, PARTS, stride=OUT_ROWS), :].T

    for slot in range(OUT_MAIN):
        ref, age = (hold_ref, sell_ref, bal_ref)[slot // AGES], slot % AGES
        rows = get(slot)
        ref[pl.ds(pace * age + half, STORES, stride=pace * AGES), :] = rows[0:STORES]
        if slot < 12:
            at = pace * (AGES * QUARTER * (slot % 4) + 3 + slot // 4) + half
            bal_ref[pl.ds(at, QUARTER, stride=pace * AGES), :] = rows[SPARE : SPARE + QUARTER]
        depots = rows[SPARE : SPARE + DEPOTS]
        if slot == OUT_DUAL_HOST:
            if half:
                depot_dual_ref[:, 0, LANES:] = depots
            else:
                depot_dual_ref[...] = depots
        if slot == OUT_ORDER_HOST:
            if half:
                ordering_ref[:, LANES:] = depots
            else:
                ordering_ref[...] = depots
    for copy in coming[1:]:
        copy.wait()
    if half:
        for i, ref in ((1, hold_ref), (2, sell_ref), (3, bal_ref)):
            ref[pl.ds(0, STORES * AGES, stride=2), :] = earlier[i][...]
        depot_dual_ref[:, 0, :LANES] = earlier[4][...]
        ordering_ref[:, :LANES] = earlier[5][...]
    for copy in going:
        copy.start()
    if half:
        coming[0].wait()
    for b in range(REGIONS):
        at = b * (LANES * pace)
        ship_ref[pl.ds(at + half, LANES, stride=pace), :] = get(OUT_MAIN + b)
        if half:
            ship_ref[pl.ds(at, LANES, stride=pace), :] = earlier[0][b * LANES : (b + 1) * LANES, :]
        if b % PIECE == PIECE - 1:
            pieces[b // PIECE].start()
    for copy in (*going, *pieces):
        copy.wait()


def tables_kernel(place_ref, store_ref, depot_ref, mask_ref, out_ref, next_ref, table, left):
    for i in range(2):
        next_ref[i] = place_ref[i]
    column = lax.broadcasted_iota(jnp.int32, (LANES, LANES), 0)

    def step(b, carry):
        for a in range(REGIONS):
            keep = mask_ref[a, pl.ds(b, 1), :] > 0
            store = jnp.where(keep, store_ref[a, pl.ds(b, 1), :], -1)
            depot = jnp.where(keep, depot_ref[a, pl.ds(b, 1), :] + DEPOT_COLUMN, -1)
            ends = (column == store) | (column == depot)
            table[b // 2, b % 2, a] = jnp.where(ends, 1.0, 0.0).astype(f32).T.astype(jnp.bfloat16)
        return carry

    lax.fori_loop(0, REGIONS, step, 0)
    going = pltpu.make_async_copy(table, out_ref, left)
    going.start()
    going.wait()


def iterations_kernel(in_ref, number_ref, table_in, *refs):
    lanes_in, out_ref, table, lanes = refs[:4], refs[4], refs[5], refs[6:10]
    slots, keeps, ship, main, aux, flow, dual, ordering, supply, packed, came, left = refs[10:]
    store_ref, depot_ref, mask_ref, cost_ref = lanes
    tables = [
        pltpu.make_async_copy(table_in.at[i], table.at[i], came.at[i]) for i in range(REGIONS // 2)
    ]
    coming = [
        pltpu.make_async_copy(lanes_in[i], lanes[i], came.at[REGIONS // 2 + i]) for i in range(4)
    ]
    for copy in (*coming, *tables):
        copy.start()
    sublane = lax.broadcasted_iota(jnp.int32, (ROWS, LANES), 0)
    first_day = sublane < SCENARIOS
    even = sublane % 2 == 0
    zero = jnp.zeros((ROWS, LANES), f32)
    quarters = [lane_window(QUARTER * q, QUARTER) for q in range(4)]
    spares = lane_window(SPARE, QUARTER)
    depot_spares = lane_window(SPARE, DEPOTS)

    def unfold(region, carry):
        at = region * (ROWS * IN_ROWS)
        for slot in range(MAIN):
            main[region, slot] = in_ref[pl.ds(at + slot, ROWS, stride=IN_ROWS), :]
        for b in range(REGIONS):
            ship[region, b] = in_ref[pl.ds(at + MAIN + b, ROWS, stride=IN_ROWS), :]
        for kind, hosts in HOSTS.items():
            total = zero
            for q in range(4):
                part = shift_lanes(main[region, hosts[q]], SPARE, QUARTER * q)
                total = jnp.where(quarters[q], part, total)
            aux[region, kind] = total
        return carry

    lax.fori_loop(0, REGIONS, unfold, 0)
    for group in range(2):
        duals, mixed = zero, zero
        for i in range(GROUP):
            region, at = group * GROUP + i, i * DEPOT_PITCH
            window = lane_window(at, DEPOTS)
            duals = jnp.where(window, shift_lanes(main[region, DUAL_HOST], SPARE, at), duals)
            mixed = jnp.where(window, shift_lanes(main[region, MIXED_HOST], SPARE, at), mixed)
        dual[group] = duals
        supply[group] = jnp.where(even, mixed, pltpu.roll(mixed, 1, 0))
        ordering[group] = jnp.where(even, pltpu.roll(mixed, ROWS - 1, 0), mixed)

    for copy in coming:
        copy.wait()
    for a in range(REGIONS):
        slots[a] = depot_ref[a] + (a % GROUP) * DEPOT_PITCH
        keeps[a] = mask_ref[a].astype(f32)
    volume, price, penalty, order_cost = (number_ref[i] for i in range(4))
    holding_cost = [number_ref[HOLDING_COST + age] for age in range(AGES)]

    def iterate(iteration, carry):
        flow[...] = jnp.zeros_like(flow)
        later = [
            dual[group] + jnp.where(first_day, other_day(dual[group]), 0.0) for group in range(2)
        ]

        def store_step(b):
            bal = [main[b, BAL + age] for age in range(AGES)]
            ddual, short = aux[b, DDUAL], aux[b, SHORT]
            new_short = jnp.maximum(0.0, short - PRIMAL_STEP * (penalty - ddual))
            aux[b, SHORT] = new_short
            sold, before, ended = zero, None, None
            for age in range(AGES):
                hold, sell = main[b, HOLD + age], main[b, SELL + age]
                rise = holding_cost[age] - bal[age]
                if age + 1 < AGES:
                    rise = rise + jnp.where(first_day, other_day(bal[age + 1]), 0.0)
                new_hold = jnp.maximum(0.0, hold - PRIMAL_STEP * rise)
                new_sell = jnp.maximum(0.0, sell - PRIMAL_STEP * (-price - bal[age] - ddual))
                main[b, HOLD + age] = new_hold
                main[b, SELL + age] = new_sell
                hold_bar = 2.0 * new_hold - hold
                sell_bar = 2.0 * new_sell - sell
                sold = sold + sell_bar
                if age == 0:
                    ended = bal[0] - DUAL_STEP * (hold_bar + sell_bar)
                else:
                    stock = jnp.broadcast_to(aux[b, STOCK, age - 1 : age, :], (ROWS, LANES))
                    carried = jnp.where(first_day, stock, other_day(before))
                    main[b, BAL + age] = bal[age] - DUAL_STEP * (hold_bar + sell_bar - carried)
                before = hold_bar
            short_bar = 2.0 * new_short - short
            aux[b, DDUAL] = ddual + DUAL_STEP * (aux[b, DEMAND] - sold - short_bar)
            return bal[0], ended

        def step(pair, carry):
            @pl.when(iteration == 0)
            def _():
                pltpu.make_async_copy(table_in.at[pair], table.at[pair], came.at[pair]).wait()

            stores = [store_step(2 * pair + i) for i in range(2)]
            arrived = [zero, zero]
            for a in range(REGIONS):
                total = None
                for i in range(2):
                    b = 2 * pair + i

                    def spread(ref):
                        return jnp.broadcast_to(ref[a, pl.ds(b, 1), :], (ROWS, LANES))

                    ends = jnp.take_along_axis(
                        stores[i][0], spread(store_ref), axis=1, mode="promise_in_bounds"
                    ) + jnp.take_along_axis(
                        later[a // GROUP], spread(slots), axis=1, mode="promise_in_bounds"
                    )
                    old = ship[a, b]
                    new = spread(keeps) * jnp.maximum(
                        0.0, old - PRIMAL_STEP * (spread(cost_ref) * volume + ends)
                    )
                    ship[a, b] = new
                    bar = 2.0 * new - old
                    high = bar.astype(jnp.bfloat16).astype(f32)
                    parts = jnp.concatenate([high, bar - high], axis=0).astype(jnp.bfloat16)
                    sums = jnp.dot(parts, table[pair, i, a], preferred_element_type=f32)
                    sums = sums[:ROWS] + sums[ROWS:]
                    arrived[i] = arrived[i] + sums
                    total = sums if i == 0 else total + sums
                flow[a] = flow[a] + total
            for i in range(2):
                main[2 * pair + i, BAL] = stores[i][1] + DUAL_STEP * arrived[i]
            return carry

        lax.fori_loop(0, REGIONS // 2, step, 0)
        for group in range(2):
            total = dual[group]
            for shift in (4, 2, 1):
                total = total + pltpu.roll(total, shift, 0)
            old = ordering[group]
            new = jnp.maximum(0.0, old - ORDER_STEP * (order_cost - total))
            ordering[group] = new
            net = -supply[group]
            for i in range(GROUP):
                at = i * DEPOT_PITCH
                part = shift_lanes(flow[group * GROUP + i], DEPOT_COLUMN, at)
                net = net + jnp.where(lane_window(at, DEPOTS), part, 0.0)
            running = net + jnp.where(first_day, 0.0, other_day(net))
            dual[group] = jnp.maximum(
                0.0, dual[group] + DEPOT_STEP * (running - (2.0 * new - old))
            )
        return carry

    lax.fori_loop(0, ITERS, iterate, 0)

    def fold(region, carry):
        at = region * (ROWS * OUT_ROWS)
        for slot in range(OUT_MAIN):
            tile = main[region, slot]
            if slot < 12:
                hosted = main[region, BAL + 3 + slot // 4]
                hosted = shift_lanes(hosted, QUARTER * (slot % 4), SPARE)
                tile = jnp.where(spares, hosted, tile)
            packed[pl.ds(at + slot, ROWS, stride=OUT_ROWS), :] = tile
        for b in range(REGIONS):
            packed[pl.ds(at + OUT_MAIN + b, ROWS, stride=OUT_ROWS), :] = ship[region, b]
        return carry

    lax.fori_loop(0, REGIONS, fold, 0)
    for group in range(2):
        for i in range(GROUP):
            region = group * GROUP + i
            at = region * (ROWS * OUT_ROWS)
            for host, ref in ((OUT_DUAL_HOST, dual), (OUT_ORDER_HOST, ordering)):
                part = shift_lanes(ref[group], i * DEPOT_PITCH, SPARE)
                packed[pl.ds(at + host, ROWS, stride=OUT_ROWS), :] = jnp.where(
                    depot_spares, part, main[region, host]
                )
    going = pltpu.make_async_copy(packed, out_ref, left)
    going.start()
    going.wait()


def swap(rows):
    parts = rows.reshape(PARTS, -1, 1, LANES)
    return lax.all_to_all(parts, EVERY, 0, 0, tiled=True).reshape(-1, LANES)


def per_device(
    shipments_init,
    holdings_init,
    selling_init,
    shortage_init,
    ordering_init,
    balance_dual_init,
    demand_dual_init,
    depot_dual_init,
    demand_base,
    demand_pattern,
    demand_index,
    initial_stock,
    depot_supply,
    lane_cost,
    item_volume,
    holding_cost,
    unit_price,
    short_penalty,
    order_cost,
    lane_depot,
    lane_store,
    lane_mask,
):
    place = jnp.stack([lax.axis_index("day"), lax.axis_index("scen")]).astype(jnp.int32)
    given = (
        shipments_init.reshape(-1, LANES),
        holdings_init.reshape(-1, LANES),
        selling_init.reshape(-1, LANES),
        balance_dual_init.reshape(-1, LANES),
        shortage_init.reshape(-1, LANES),
        demand_dual_init.reshape(-1, LANES),
        demand_base,
        demand_pattern,
        demand_index.reshape(1, STORES),
        jnp.transpose(initial_stock, (1, 0, 2)),
        depot_dual_init.reshape(DEPOTS, 1, SKUS),
        ordering_init,
        depot_supply,
    )
    table_shape = (REGIONS // 2, 2, REGIONS, LANES, LANES)
    tiles = (REGIONS, REGIONS, LANES)
    arrived = []
    for half in range(HALVES):
        packed = call(
            functools.partial(pack_kernel, half),
            pltpu.HBM((PARTS * IN_ROWS, LANES), f32),
            [SM] + [HB] * len(given),
            HB,
            scratch=[
                *(pltpu.VMEM(array.shape, array.dtype) for array in given),
                pltpu.VMEM((PARTS * IN_ROWS, LANES), f32),
                pltpu.VMEM((MAIN, LANES, LANES), f32),
                pltpu.VMEM((8, LANES), jnp.int32),
                pltpu.SemaphoreType.DMA((len(given),)),
                pltpu.SemaphoreType.DMA,
            ],
            micros=4,
        )(place, *(in_hbm(array) for array in given))
        arrived.append(swap(packed))
        if half == 0:
            table, place = call(
                tables_kernel,
                (pltpu.HBM(table_shape, jnp.bfloat16), jax.ShapeDtypeStruct((2,), jnp.int32)),
                [SM, VM, VM, VM],
                (HB, SM),
                scratch=[pltpu.VMEM(table_shape, jnp.bfloat16), pltpu.SemaphoreType.DMA],
                micros=5,
            )(place, lane_store, lane_depot, lane_mask)
    numbers = jnp.concatenate(
        [jnp.stack([item_volume, unit_price, short_penalty, order_cost]), holding_cost], axis=0
    )
    own = (lax.axis_index("region") * DAYS + lax.axis_index("day")) * SCENARIOS
    own = own + lax.axis_index("scen")
    back = []
    for half in range(HALVES):
        mine = lax.dynamic_slice(numbers, (0, half * LANES + own), (numbers.shape[0], 1))
        back.append(
            swap(
                call(
                    iterations_kernel,
                    pltpu.HBM((PARTS * OUT_ROWS, LANES), f32),
                    [VM, SM] + [HB] * 5,
                    HB,
                    scratch=[
                        pltpu.VMEM(table_shape, jnp.bfloat16),
                        *[pltpu.VMEM(tiles, jnp.int32)] * 3,
                        pltpu.VMEM(tiles, f32),
                        pltpu.VMEM(tiles, jnp.int32),
                        pltpu.VMEM(tiles, f32),
                        pltpu.VMEM((REGIONS, REGIONS, ROWS, LANES), f32),
                        pltpu.VMEM((REGIONS, MAIN, ROWS, LANES), f32),
                        pltpu.VMEM((REGIONS, AUX, ROWS, LANES), f32),
                        pltpu.VMEM((REGIONS, ROWS, LANES), f32),
                        pltpu.VMEM((2, ROWS, LANES), f32),
                        pltpu.VMEM((2, ROWS, LANES), f32),
                        pltpu.VMEM((2, ROWS, LANES), f32),
                        pltpu.VMEM((PARTS * OUT_ROWS, LANES), f32),
                        pltpu.SemaphoreType.DMA((REGIONS // 2 + 4,)),
                        pltpu.SemaphoreType.DMA,
                    ],
                    micros=20,
                )(
                    arrived[half],
                    mine.reshape(-1),
                    *(
                        in_hbm(array)
                        for array in (table, lane_store, lane_depot, lane_mask, lane_cost)
                    ),
                )
            )
        )
    done = ()
    for half in range(HALVES):
        pace = half + 1
        flat = (STORES * pace * AGES, LANES)
        shapes = (
            (pace * REGIONS * LANES, LANES),
            flat,
            flat,
            flat,
            (DEPOTS, 1, SKUS) if half else (DEPOTS, LANES),
            (DEPOTS, pace * LANES),
        )
        count = len(shapes)
        done = call(
            functools.partial(unpack_kernel, half),
            tuple(pltpu.HBM(shape, f32) for shape in shapes),
            [VM] + [HB] * len(done),
            (HB,) * count,
            scratch=[
                *(pltpu.VMEM(shape, f32) for shape in shapes),
                *(pltpu.VMEM(array.shape, f32) for array in done),
                pltpu.SemaphoreType.DMA((count,)),
                pltpu.SemaphoreType.DMA((count + REGIONS // PIECE,)),
            ],
            micros=4,
        )(in_vmem(back[half]) if half else back[half], *(in_hbm(array) for array in done))
    shipments, holdings, selling, balance, depot_dual, ordering = done
    return (
        shipments.reshape(1, 1, REGIONS, LANES, 1, SKUS),
        holdings.reshape(1, STORES, 1, AGES, SKUS),
        selling.reshape(1, STORES, 1, AGES, SKUS),
        ordering,
        balance.reshape(1, STORES, 1, AGES, SKUS),
        depot_dual.reshape(1, DEPOTS, 1, SKUS),
    )


def solution(mesh):
    placed = (
        P("scen", "region", None, None, "day", None),
        P("scen", "region", "day", None, None),
        P("scen", "region", "day", None, None),
        P("scen", "region", "day", None),
        P("region", None),
        P("scen", "region", "day", None, None),
        P("scen", "region", "day", None),
        P("scen", "region", "day", None),
        P("region", None),
        P(),
        P("scen", "region", "day"),
        P("region", None, None),
        P("region", "day", None),
        P(),
        P(),
        P(),
        P(),
        P(),
        P(),
        P(),
        P(),
        P(),
    )
    return jax.shard_map(
        per_device,
        mesh=mesh,
        in_specs=placed,
        out_specs=(
            P("scen", "region", None, None, "day", None),
            P("scen", "region", "day", None, None),
            P("scen", "region", "day", None, None),
            P("region", None),
            P("scen", "region", "day", None, None),
            P("scen", "region", "day", None),
        ),
        check_vma=False,
    )
```
